32 devices in a mesh: ctx: 4 (over x, core), fsdp: 8 (over z, y).
Axes of the slice: x: 2, y: 2, z: 4, core: 2. Of those that a mesh axis runs over, the one named last changes fastest.
Arguments:
- hidden_in: bfloat16 [2, 2, 4, 512, 2048], P(None, None, 'ctx', 'fsdp'), may hold values from -6 to 6
- cotangent: bfloat16 [2, 2, 4, 512, 2048], P(None, None, 'ctx', 'fsdp'), may hold values from -6 to 6
- routes: int32 [2, 2, 4, 512, 4], P(None, None, 'ctx', 'fsdp'), may hold values from 0 to 7, all different within a row
- priority: int32 [2, 2, 4, 512], P(None, None, 'ctx', 'fsdp'), may hold values from 0 to 1048575
- gain_attn: bfloat16 [2048], P('fsdp'), may hold values from 0.5 to 1.5
- attention_input_weights: bfloat16 [3, 2048, 2048], P(None, None, 'fsdp'), may hold values from -0.125 to 0.125
- attention_output_weights: bfloat16 [2048, 2048], P('fsdp'), may hold values from -0.5 to 0.5
- gain_ffn: bfloat16 [2048], P('fsdp'), may hold values from 0.5 to 1.5
- router: bfloat16 [2048, 8], P('fsdp'), may hold values from -0.0625 to 0.0625
- shared_gate: bfloat16 [2048], P('fsdp'), may hold values from -0.125 to 0.125
- shared_in: bfloat16 [2, 5632, 2048], P(None, 'fsdp'), may hold values from -0.125 to 0.125
- shared_out: bfloat16 [5632, 2048], P('fsdp'), may hold values from -0.15625 to 0.15625
- expert_in: bfloat16 [8, 2, 1408, 2048], P(None, None, 'fsdp'), may hold values from -0.125 to 0.125
- expert_out: bfloat16 [8, 1408, 2048], P(None, 'fsdp'), may hold values from -0.3125 to 0.3125
Outputs:
- layer_out: bfloat16 [2, 2, 4, 512, 2048], P(None, None, 'ctx', 'fsdp')
- grad_hidden: bfloat16 [2, 2, 4, 512, 2048], P(None, None, 'ctx', 'fsdp')
- grad_gain_attn: float32 [2048], P('fsdp')
- grad_attn_in: float32 [3, 2048, 2048], P(None, None, 'fsdp')
- grad_attn_out: float32 [2048, 2048], P('fsdp')
- grad_gain_ffn: float32 [2048], P('fsdp')
- grad_router: float32 [2048, 8], P('fsdp')
- grad_shared_gate: float32 [2048], P('fsdp')
- grad_shared_in: float32 [2, 5632, 2048], P(None, 'fsdp')
- grad_shared_out: float32 [5632, 2048], P('fsdp')
- grad_expert_in: float32 [8, 2, 1408, 2048], P(None, None, 'fsdp')
- grad_expert_out: float32 [8, 1408, 2048], P(None, 'fsdp')
The draws below stay inside these ranges and needn't reach their ends.
Inputs may be any that keep to these rules, and one draw needn't show every extreme that they name: `routes`: each token names 4 different experts.
All inputs are finite; a program needn't handle non-finite values.
Results may differ from the reference program's by a relative error of at most 0.025.
Values may be sent and summed in bfloat16 or wider, within the bound.
A program may use at most 640 MiB of HBM per device.

```python
from functools import partial
import jax
import jax.numpy as jnp
from jax import lax

D = 2048
HEADS = 16
HEAD_DIM = 128
FF = 1408
SHARED = 5632
TOP = 4
EXPERTS = 8
BLOCK = 256
SPAN = 512
SEQS = 2
SEQ_LEN = 4096
CAP = 160
N_CTX = 4
N_FSDP = 8


def touch_ends(values, rng, low, high):
    shape = values.shape
    place = [jax.random.randint(jax.random.fold_in(rng, axis), (), 0, shape[axis]) for axis in range(len(shape))]
    values = values.at[tuple(place)].set(low)
    longest = shape.index(max(shape))
    place[longest] = (place[longest] + 1) % shape[longest]
    return values.at[tuple(place)].set(high)


def levels(own_key, extent, shards, smallest, high):
    level, own = 1.0, jax.random.fold_in(own_key, 6)
    for dim, shards_of in shards:
        heights = jnp.exp(jax.random.uniform(jax.random.fold_in(own, dim), (shards_of,), jnp.float32, smallest / len(shards), high / len(shards)))
        level = level * jnp.repeat(heights, extent[dim] // shards_of).reshape([-1 if axis == dim else 1 for axis in range(len(extent))])
    return level


def distinct(rng, rows, number_of, top, lift):
    order = jax.random.permutation(jax.random.fold_in(rng, 1), number_of)
    pull = order
    for power in range(3):
        pull = pull * pull // number_of
    pull = pull * lift // number_of
    chance = jax.random.randint(jax.random.fold_in(rng, 2), (rows, number_of), 0, 4096) + pull
    holders = jax.random.permutation(jax.random.fold_in(rng, 3), rows)[jnp.arange(number_of) % rows]
    chance = jnp.where(jnp.arange(rows)[:, None] == holders[None, :], 1 << 14, chance)
    merit = chance * number_of + jnp.arange(number_of)
    return lax.top_k(merit.astype(jnp.int32), top)[1].astype(jnp.int32)


def bell_draw(rng, shape, width, limit, cuts=(), held_as=jnp.bfloat16):
    drawn = jax.random.normal(rng, shape, jnp.float32) * width
    if len(cuts) > 0:
        drawn = levels(rng, shape, cuts, -0.22, 0.18) * drawn
    return jnp.clip(drawn, min=-limit, max=limit).astype(held_as)


def setup_inputs(seed: int = 0) -> dict:
    streams_of = jax.random.split(jax.random.key(seed), 15)
    return {
        "hidden_in": bell_draw(streams_of[0], (SEQS, 2, N_CTX, SPAN, D), 1.0, 6.0, ((2, 4), (3, 8))),
        "cotangent": bell_draw(streams_of[1], (SEQS, 2, N_CTX, SPAN, D), 1.0, 6.0, ((2, 4), (3, 8))),
        "routes": distinct(streams_of[2], SEQS * 2 * N_CTX * SPAN, EXPERTS, TOP, 4096).reshape((SEQS, 2, N_CTX, SPAN, TOP)),
        "priority": touch_ends(jax.random.randint(streams_of[3], (SEQS, 2, N_CTX, SPAN), 0, 1048576), jax.random.fold_in(streams_of[3], 1), 0, 1048575).astype(jnp.int32),
        "gain_attn": jnp.clip(1.0 + 0.1 * jax.random.normal(streams_of[4], (D,), jnp.float32), 0.5, 1.5).astype(jnp.bfloat16),
        "attention_input_weights": bell_draw(streams_of[5], (3, D, D), D ** -0.5, 0.125, ((2, 8),)),
        "attention_output_weights": bell_draw(streams_of[6], (D, D), (D // 16) ** -0.5, 0.5, ((0, 8),)),
        "gain_ffn": jnp.clip(1.0 + 0.1 * jax.random.normal(streams_of[7], (D,), jnp.float32), 0.5, 1.5).astype(jnp.bfloat16),
        "router": bell_draw(streams_of[8], (D, EXPERTS), (4 * D) ** -0.5, 0.0625, ((0, 8),)),
        "shared_gate": bell_draw(streams_of[9], (D,), D ** -0.5, 0.125, ((0, 8),)),
        "shared_in": bell_draw(streams_of[10], (2, SHARED, D), D ** -0.5, 0.125, ((1, 8),)),
        "shared_out": bell_draw(streams_of[11], (SHARED, D), (SHARED // 4) ** -0.5, 0.15625, ((0, 8),)),
        "expert_in": bell_draw(streams_of[12], (EXPERTS, 2, FF, D), D ** -0.5, 0.125, ((2, 8),)),
        "expert_out": bell_draw(streams_of[13], (EXPERTS, FF, D), (FF // 4) ** -0.5, 0.3125, ((1, 8),)),
    }


EPSILON = 1e-06
ROPE_BASE = 1000000.0
MASKED = -1e+30
EXACT_PRECISION = lax.Precision.HIGHEST

@jax.custom_vjp
def low(v):
    return lax.optimization_barrier(v.astype(jnp.bfloat16)).astype(jnp.float32)

@jax.custom_vjp
def low_back(v):
    return v

def low_keep(v):
    return (low(v), None)

def low_pass(kept, grad):
    return (grad,)

def back_keep(v):
    return (v, None)

def back_low(kept, grad):
    return (low(grad),)
low.defvjp(low_keep, low_pass)
low_back.defvjp(back_keep, back_low)

def rope_tables(positions, head_size):
    halves = jnp.arange(head_size // 2, dtype=jnp.float32)
    frequency = ROPE_BASE ** (-2.0 * halves / head_size)
    angles = positions.astype(jnp.float32)[:, None] * frequency[None, :]
    return (jnp.cos(angles), jnp.sin(angles))

def rotate(values, cosine, sine, direction):
    middle = values.shape[-1] // 2
    first_half = values[..., :middle]
    second_half = values[..., middle:]
    cos_rows = cosine[:, None, :]
    sin_rows = sine[:, None, :] * direction
    return jnp.concatenate([first_half * cos_rows - second_half * sin_rows, second_half * cos_rows + first_half * sin_rows], axis=-1)

def rms_scale(values, gain):
    return values * lax.rsqrt(lax.optimization_barrier(jnp.mean(values * values, axis=-1, keepdims=True)) + EPSILON) * gain

def dispatch_table(route_rows, order_keys, experts, capacity):
    count = order_keys.shape[0]
    row_index = jnp.arange(count, dtype=jnp.int32)
    before = (order_keys[None, :] < order_keys[:, None]) | (order_keys[None, :] == order_keys[:, None]) & (row_index[None, :] < row_index[:, None])
    chosen = route_rows[:, :, None] == jnp.arange(experts, dtype=jnp.int32)[None, None, :]
    naming = lax.optimization_barrier(jnp.sum(chosen.astype(jnp.int32), axis=1, dtype=jnp.int32))
    ahead = jnp.dot(before.astype(jnp.int32), naming)
    slots = lax.optimization_barrier(jnp.sum(jnp.where(chosen, ahead[:, None, :], 0), axis=2, dtype=jnp.int32))
    placed = slots[:, :, None] == jnp.arange(capacity, dtype=jnp.int32)[None, None, :]
    return jnp.einsum('rke,rkc->ecr', chosen.astype(jnp.float32), placed.astype(jnp.float32))

def to_sequence(dealt):
    joined = jnp.concatenate([dealt[:, 0], jnp.flip(dealt[:, 1], axis=1)], axis=1)
    return joined.reshape((joined.shape[0], -1) + joined.shape[3:])

def to_dealt(ordered):
    blocks = ordered.reshape((ordered.shape[0], 2 * N_CTX, SPAN) + ordered.shape[2:])
    return jnp.stack([blocks[:, :N_CTX], jnp.flip(blocks[:, N_CTX:], axis=1)], axis=1)

def to_groups(dealt):
    tail = dealt.shape[4:]
    split = dealt.reshape((SEQS, 2, N_CTX, N_FSDP, SPAN // N_FSDP) + tail)
    moved = jnp.moveaxis(split, (2, 3), (0, 1))
    return moved.reshape((N_CTX * N_FSDP, SEQS * 2 * (SPAN // N_FSDP)) + tail)

def from_groups(grouped):
    tail = grouped.shape[2:]
    split = grouped.reshape((N_CTX, N_FSDP, SEQS, 2, SPAN // N_FSDP) + tail)
    moved = jnp.moveaxis(split, (0, 1), (2, 3))
    return moved.reshape((SEQS, 2, N_CTX, SPAN) + tail)

def attend_block(query_rows, key_rows, value_rows, first_row):
    scores = low_back(jnp.einsum('qhd,khd->hqk', query_rows, key_rows, precision=EXACT_PRECISION) * HEAD_DIM ** (-0.5))
    query_block = (first_row + jnp.arange(query_rows.shape[0], dtype=jnp.int32)) // BLOCK
    key_block = jnp.arange(key_rows.shape[0], dtype=jnp.int32) // BLOCK
    allowed = key_block[None, :] <= query_block[:, None]
    scores = jnp.where(allowed[None], scores, MASKED)
    weights = jax.nn.softmax(scores, axis=-1)
    return jnp.einsum('hqk,khd->qhd', low(weights), value_rows, precision=EXACT_PRECISION)

def attend_sequence(sequence_items):
    query_seq, key_seq, value_seq = sequence_items
    pieces = query_seq.reshape(N_CTX, 2 * SPAN, HEADS, HEAD_DIM)
    starts = jnp.arange(N_CTX, dtype=jnp.int32) * (2 * SPAN)

    def one_piece(piece_pair):
        return attend_block(piece_pair[0], key_seq, value_seq, piece_pair[1])
    return lax.map(jax.checkpoint(one_piece), (pieces, starts)).reshape(query_seq.shape)

def feed_forward(rows_in, inner, outer):
    gate_val = low_back(jnp.einsum('...d,fd->...f', rows_in, inner[0], precision=EXACT_PRECISION))
    up_val = low_back(jnp.einsum('...d,fd->...f', rows_in, inner[1], precision=EXACT_PRECISION))
    activated = low(jax.nn.silu(gate_val) * up_val)
    return low_back(jnp.einsum('...f,fd->...d', activated, outer, precision=EXACT_PRECISION))

def expert_group(expert_in, expert_out, group_items):
    table, token_rows, group_gates = group_items
    buffers = jnp.einsum('ecr,rd->ecd', table, token_rows, precision=EXACT_PRECISION)
    gate_val = low_back(jnp.einsum('ecd,efd->ecf', buffers, expert_in[:, 0], precision=EXACT_PRECISION))
    up_val = low_back(jnp.einsum('ecd,efd->ecf', buffers, expert_in[:, 1], precision=EXACT_PRECISION))
    activated = low(jax.nn.silu(gate_val) * up_val)
    results = low_back(jnp.einsum('ecf,efd->ecd', activated, expert_out, precision=EXACT_PRECISION))
    picked = jnp.einsum('ecr,ecd->erd', table, results, precision=EXACT_PRECISION)
    return jnp.einsum('re,erd->rd', group_gates, picked, precision=EXACT_PRECISION)

def layer_forward(tables, hidden_in, gain_attn, attention_input_weights, attention_output_weights, gain_ffn, router, shared_gate, shared_in, shared_out, expert_in, expert_out):
    normed_one = low(rms_scale(hidden_in, gain_attn))
    sequence_input = to_sequence(normed_one)
    projected_rows = jnp.einsum('tmn,hnq->htmq', sequence_input, attention_input_weights, precision=EXACT_PRECISION)
    shaped = projected_rows.reshape(3, SEQS, SEQ_LEN, HEADS, HEAD_DIM)
    cosine, sine = rope_tables(jnp.arange(SEQ_LEN, dtype=jnp.int32), HEAD_DIM)
    query = low(rotate(low_back(shaped[0]), cosine, sine, 1.0))
    key_rows = low(rotate(low_back(shaped[1]), cosine, sine, 1.0))
    value_rows = low(low_back(shaped[2]))
    mixed_result = lax.map(attend_sequence, (query, key_rows, value_rows))
    mixed_result = low(low_back(mixed_result)).reshape(SEQS, SEQ_LEN, D)
    attention_contribution = low_back(jnp.einsum('yiw,wa->yia', mixed_result, attention_output_weights, precision=EXACT_PRECISION))
    resid_mid = hidden_in + to_dealt(attention_contribution)
    normed_two = low(rms_scale(resid_mid, gain_ffn))
    logits = low_back(jnp.einsum('...d,de->...e', normed_two, router, precision=EXACT_PRECISION))
    gates = jax.nn.softmax(logits, axis=-1)
    shared_weight = jax.nn.sigmoid(jnp.einsum('...d,d->...', normed_two, shared_gate, precision=EXACT_PRECISION))
    shared_part = feed_forward(normed_two, shared_in, shared_out)
    grouped = lax.map(jax.checkpoint(partial(expert_group, expert_in, expert_out)), (tables, to_groups(normed_two), to_groups(gates)))
    return resid_mid + from_groups(grouped) + shared_weight[..., None] * shared_part

def reference(hidden_in, cotangent, routes, priority, gain_attn, attention_input_weights, attention_output_weights, gain_ffn, router, shared_gate, shared_in, shared_out, expert_in, expert_out):
    tables = jax.vmap(partial(dispatch_table, experts=EXPERTS, capacity=CAP))(to_groups(routes), to_groups(priority))
    inputs = tuple((value.astype(jnp.float32) for value in (hidden_in, gain_attn, attention_input_weights, attention_output_weights, gain_ffn, router, shared_gate, shared_in, shared_out, expert_in, expert_out)))
    result, pullback = jax.vjp(partial(layer_forward, tables), *inputs)
    grads = pullback(cotangent.astype(jnp.float32))
    return (result.astype(jnp.bfloat16), grads[0].astype(jnp.bfloat16), grads[1], grads[2], grads[3], grads[4], grads[5], grads[6], grads[7], grads[8], grads[9], grads[10])
```

```python
import functools

import jax
import jax.numpy as jnp
import numpy as np
from jax import lax
from jax.experimental import pallas as pl
from jax.experimental.pallas import tpu as pltpu
from jax.sharding import PartitionSpec as P

HEAD_DIM = 128
BLOCK = 256
EPSILON = 1e-06
ROPE_BASE = 1000000.0
LOG2E = 1.4426950408889634
EXACT = lax.Precision.HIGHEST
BF = jnp.bfloat16
F32 = jnp.float32
MIB = 1 << 20


def ring_order(count):
    if count == 8:
        return [0, 2, 4, 6, 7, 5, 3, 1]
    side = int(round(count**0.5))
    if side * side != count:
        return list(range(count))
    order = []
    for row in range(side):
        line = [row * side + col for col in range(side)]
        order += line if row % 2 == 0 else line[::-1]
    return order


def after(value, *others):
    return lax.optimization_barrier((value, *others))[0]


def dot(a, b, ca, cb):
    return lax.dot_general(a, b, (((ca,), (cb,)), ((), ())), preferred_element_type=F32)


def project_kernel(h_ref, gain_ref, w_ref, cos_ref, sin_ref, n_ref, q_ref, kv_ref):
    x = h_ref[...].astype(F32)
    inverse = lax.rsqrt(jnp.mean(x * x, axis=-1, keepdims=True) + EPSILON)
    normed = (x * inverse * gain_ref[...]).astype(BF)
    n_ref[...] = normed
    cosine, sine = cos_ref[...], sin_ref[...]
    seqs, _, _, blocks, pr, _ = kv_ref.shape
    for j in range(3):
        y = dot(normed, w_ref[j], 1, 0)
        for lo in range(0, y.shape[1], HEAD_DIM):
            cols = slice(lo, lo + HEAD_DIM)
            part = y[:, cols]
            if j < 2:
                part = part * cosine + pltpu.roll(part, HEAD_DIM // 2, 1) * sine
            part = part.astype(BF)
            if j == 0:
                q_ref[:, cols] = part
            else:
                for b in range(blocks):
                    for s in range(seqs):
                        at = (b * seqs + s) * pr
                        kv_ref[s, j - 1, 0, b, :, cols] = part[at : at + pr]


def project(rows, gain, weights, cosine, sine, seqs, n):
    count, width = rows.shape
    local = weights.shape[2]
    tile = 256
    pr = count // (2 * n * seqs)
    blocks = tile // (seqs * pr)
    per_span = n // blocks
    row = lambda w: pl.BlockSpec((tile, w), lambda i: (i, 0))
    return pl.pallas_call(
        project_kernel,
        grid=(count // tile,),
        in_specs=[
            row(width),
            pl.BlockSpec((1, width), lambda i: (0, 0)),
            pl.BlockSpec((3, width, local), lambda i: (0, 0, 0)),
            row(HEAD_DIM),
            row(HEAD_DIM),
        ],
        out_specs=[
            row(width),
            row(local),
            pl.BlockSpec(
                (seqs, 2, 1, blocks, pr, local),
                lambda i: (0, 0, i // per_span, lax.rem(i, per_span), 0, 0),
            ),
        ],
        out_shape=[
            jax.ShapeDtypeStruct((count, width), BF),
            jax.ShapeDtypeStruct((count, local), BF),
            jax.ShapeDtypeStruct((seqs, 2, 2, n, pr, local), BF),
        ],
        compiler_params=pltpu.CompilerParams(vmem_limit_bytes=40 * MIB),
        cost_estimate=pl.CostEstimate(
            flops=6 * count * width * local, bytes_accessed=4 * count * width, transcendentals=0
        ),
        name="project",
    )(rows, gain, weights, cosine, sine)


def relative(c, other, ctx_count):
    lanes = ctx_count // 2
    apart = lax.rem(c // 2 - other // 2 + lanes, lanes)
    return apart * 2 + lax.rem(c + other, 2)


def attend_kernel(ctx_count, c_ref, q_ref, k_ref, v_ref, fc_ref, fr_ref, *refs):
    o_ref, lse_ref = refs[-2:]
    c = c_ref[0]
    kind = pl.program_id(1)
    q = q_ref[...].reshape(k_ref.shape[3:])
    scale = HEAD_DIM**-0.5 * LOG2E

    def diag():
        s = dot(q, k_ref[0, 0, kind], 1, 1) * scale
        s = jnp.where(fr_ref[0] <= fc_ref[0], s, -1e30)
        m = jnp.max(s, axis=-1, keepdims=True)
        p = jnp.exp2(s - m)
        return m, jnp.sum(p, axis=-1, keepdims=True), dot(p.astype(BF), v_ref[0, 0, kind], 1, 0)

    def step(other, pp, state):
        m, l, acc = state
        j = relative(c, other, ctx_count)
        s = dot(q, k_ref[j, 0, pp], 1, 1) * scale
        m_new = jnp.maximum(m, jnp.max(s, axis=-1, keepdims=True))
        p = jnp.exp2(s - m_new)
        a = jnp.exp2(m - m_new)
        return (
            m_new,
            l * a + jnp.sum(p, axis=-1, keepdims=True),
            acc * a + dot(p.astype(BF), v_ref[j, 0, pp], 1, 0),
        )

    state = diag()
    state = lax.fori_loop(
        0, jnp.where(kind == 0, c, ctx_count), lambda i, st: step(i, 0, st), state
    )
    state = lax.fori_loop(
        jnp.where(kind == 0, ctx_count, c + 1), ctx_count, lambda i, st: step(i, 1, st), state
    )
    m, l, acc = state
    o_ref[...] = (acc / l).astype(BF).reshape(o_ref.shape)
    lse = jnp.broadcast_to(m + jnp.log2(l), acc.shape)
    lse_ref[0, 0] = jnp.transpose(lse)[:8]


def attend(c, q, kv, seq, flag_col, flag_row, out):
    ctx_count, _, _, span, local = kv.shape
    heads = local // HEAD_DIM
    _, n, _, pr, _ = q.shape
    block = (ctx_count, 1, 2, span, HEAD_DIM)
    ks = pl.BlockSpec(block, lambda h, t, c: (0, 0, 0, 0, h))
    vs = pl.BlockSpec(block, lambda h, t, c: (0, 1, 0, 0, h))
    qs = pl.BlockSpec((1, n, 1, pr, HEAD_DIM), lambda h, t, c: (t, 0, seq, 0, h))
    held = [] if out is None else [out]
    return pl.pallas_call(
        functools.partial(attend_kernel, ctx_count),
        grid_spec=pltpu.PrefetchScalarGridSpec(
            num_scalar_prefetch=1,
            grid=(heads, 2),
            in_specs=[
                qs,
                ks,
                vs,
                pl.BlockSpec((1, span, 1), lambda h, t, c: (t, 0, 0)),
                pl.BlockSpec((1, 1, span), lambda h, t, c: (t, 0, 0)),
            ]
            + [pl.BlockSpec(memory_space=pl.ANY)] * len(held),
            out_specs=[qs, pl.BlockSpec((1, 1, 8, span), lambda h, t, c: (h, t, 0, 0))],
        ),
        out_shape=[
            jax.ShapeDtypeStruct(q.shape, BF),
            jax.ShapeDtypeStruct((heads, 2, 8, span), F32),
        ],
        input_output_aliases={6: 0} if held else {},
        compiler_params=pltpu.CompilerParams(vmem_limit_bytes=48 * MIB),
        cost_estimate=pl.CostEstimate(
            flops=heads * 9 * 8 * span * span * HEAD_DIM, bytes_accessed=8 * MIB, transcendentals=0
        ),
        name="attend",
    )(c, q, kv, kv, flag_col, flag_row, *held)


def attend_back_kernel(
    ctx_count,
    c_ref,
    q_ref,
    k_ref,
    v_ref,
    do_ref,
    o_ref,
    lse_ref,
    cos_ref,
    sin_ref,
    fc_ref,
    fr_ref,
    *refs,
):
    dq_ref, dkv_ref, dk_acc, dv_acc, dq_acc = refs[-5:]
    flat = (k_ref.shape[3], k_ref.shape[4])
    c = c_ref[0]
    root = HEAD_DIM**-0.5
    dk_acc[...] = jnp.zeros_like(dk_acc)
    dv_acc[...] = jnp.zeros_like(dv_acc)
    for kind in range(2):
        q, do = q_ref[kind].reshape(flat), do_ref[kind].reshape(flat)
        product = do.astype(F32) * o_ref[kind].reshape(flat).astype(F32)
        delta = jnp.sum(jnp.transpose(product), axis=0, keepdims=True)
        lse = lse_ref[0, kind, 0:1]
        dq_acc[...] = jnp.zeros_like(dq_acc)

        def step(j, pp, masked, q=q, do=do, delta=delta, lse=lse, kind=kind):
            k, v = k_ref[j, 0, pp], v_ref[j, 0, pp]
            s = dot(k, q, 1, 1) * (root * LOG2E)
            if masked:
                s = jnp.where(fc_ref[kind] <= fr_ref[kind], s, -1e30)
            p = jnp.exp2(s - lse)
            dp = dot(v, do, 1, 1)
            ds = (p * (dp - delta)).astype(BF)
            dv_acc[j, pp] += dot(p.astype(BF), do, 1, 0)
            dk_acc[j, pp] += dot(ds, q, 1, 0)
            dq_acc[...] += dot(ds, k, 0, 0)

        step(0, kind, True)

        def plain(i, carry, pp):
            step(relative(c, i, ctx_count), pp, False)
            return carry

        if kind == 0:
            lax.fori_loop(0, c, functools.partial(plain, pp=0), 0)
        else:
            lax.fori_loop(0, ctx_count, functools.partial(plain, pp=0), 0)
            lax.fori_loop(c + 1, ctx_count, functools.partial(plain, pp=1), 0)
        dq = dq_acc[...] * root
        cosine, sine = cos_ref[kind].reshape(flat), sin_ref[kind].reshape(flat)
        dq = dq * cosine - pltpu.roll(dq, HEAD_DIM // 2, 1) * sine
        dq_ref[kind] = dq.astype(BF).reshape(dq_ref.shape[1:])
    dkv_ref[:, 0] = (dk_acc[...] * root).astype(BF)
    dkv_ref[:, 1] = dv_acc[...].astype(BF)


def attend_back(c, q, kv, do, o, lse, seq, cosine, sine, flag_col, flag_row, out, *deps):
    ctx_count, _, _, span, local = kv.shape
    heads = local // HEAD_DIM
    _, n, _, pr, _ = q.shape
    block = (ctx_count, 1, 2, span, HEAD_DIM)
    ks = pl.BlockSpec(block, lambda h, c: (0, 0, 0, 0, h))
    vs = pl.BlockSpec(block, lambda h, c: (0, 1, 0, 0, h))
    qs = pl.BlockSpec((2, n, 1, pr, HEAD_DIM), lambda h, c: (0, 0, seq, 0, h))
    table = pl.BlockSpec((2, n, 1, pr, HEAD_DIM), lambda h, c: (0, 0, seq, 0, 0))
    kv_out = pl.BlockSpec((ctx_count, 2, 2, span, HEAD_DIM), lambda h, c: (0, 0, 0, 0, h))
    held = ([] if out is None else [out]) + list(deps)
    return pl.pallas_call(
        functools.partial(attend_back_kernel, ctx_count),
        grid_spec=pltpu.PrefetchScalarGridSpec(
            num_scalar_prefetch=1,
            grid=(heads,),
            in_specs=[
                qs,
                ks,
                vs,
                qs,
                qs,
                pl.BlockSpec((1, 2, 8, span), lambda h, c: (h, 0, 0, 0)),
                table,
                table,
                pl.BlockSpec((2, span, 1), lambda h, c: (0, 0, 0)),
                pl.BlockSpec((2, 1, span), lambda h, c: (0, 0, 0)),
            ]
            + [pl.BlockSpec(memory_space=pl.ANY)] * len(held),
            out_specs=[qs, kv_out],
            scratch_shapes=[
                pltpu.VMEM((ctx_count, 2, span, HEAD_DIM), F32),
                pltpu.VMEM((ctx_count, 2, span, HEAD_DIM), F32),
                pltpu.VMEM((span, HEAD_DIM), F32),
            ],
        ),
        out_shape=[jax.ShapeDtypeStruct(q.shape, BF), jax.ShapeDtypeStruct(kv.shape, BF)],
        input_output_aliases={} if out is None else {11: 0},
        compiler_params=pltpu.CompilerParams(vmem_limit_bytes=56 * MIB),
        cost_estimate=pl.CostEstimate(
            flops=heads * 9 * 20 * span * span * HEAD_DIM, bytes_accessed=12 * MIB, transcendentals=0
        ),
        name="attend_back",
    )(c, q, kv, kv, do, o, lse, cosine, sine, flag_col, flag_row, *held)


def merge_kernel(n, ctx_count, c_ref, shard_ref, *refs):
    a_refs, b_refs, refs = refs[:n], refs[n : 2 * n], refs[2 * n :]
    pieces, refs = refs[:ctx_count], refs[ctx_count:]
    h_ref, gain_ref, r_ref, n_ref, own_ref, logit_ref, w_ref, mixed_ref, wide = refs
    i = pl.program_id(0)
    c = c_ref[0]
    count, local = wide.shape[0], wide.shape[1] // n
    own, tile, share = count // n, h_ref.shape[0], local // ctx_count
    per_span = count // tile

    @pl.when(i == 0)
    def _():
        half = ctx_count // 2
        for j in range(ctx_count):
            other = lax.rem(c // 2 - j // 2 + half, half) * 2 + lax.rem(c + j, 2)
            at = pl.multiple_of(other * share, share)
            for k in range(n):
                w_ref[k, pl.ds(at, share), :] = pieces[j][shard_ref[k]]

    def turned(ref, k, by):
        cols = slice(k * local, (k + 1) * local)
        wide[by * own :, cols] = ref[: count - by * own]
        if by:
            wide[: by * own, cols] = ref[count - by * own : count]

    @pl.when(i == 0)
    def _():
        for k in range(n):
            turned(a_refs[k], k, k)

    @pl.when(i == per_span)
    def _():
        for k in range(n):
            turned(b_refs[-k % n], k, -k % n)

    part = lax.rem(i, per_span)
    rows = wide[pl.ds(pl.multiple_of(part * tile, tile), tile), :]
    weights = w_ref[...].reshape(n * local, w_ref.shape[2])
    resid = h_ref[...].astype(F32) + dot(rows, weights, 1, 0)
    inverse = lax.rsqrt(jnp.mean(resid * resid, axis=-1, keepdims=True) + EPSILON)
    normed = (resid * inverse * gain_ref[...]).astype(BF)
    n_ref[...] = normed
    logit_ref[...] = dot(r_ref[...], normed, 1, 1)

    @pl.when(part == 0)
    def _():
        own_ref[0] = resid[:own]
        mixed_ref[0] = rows[:own]


def merge(c, shards, got_a, got_b, pieces, rows, gain, router_t):
    count, width = rows.shape
    n, ctx_count = len(got_a), len(pieces)
    span, local = got_b[0].shape
    tile = 256
    per_span, own = span // tile, span // n
    once = pl.Buffered(1)
    row = pl.BlockSpec((tile, width), lambda i, c, f: (i, 0))
    own_rows = pl.BlockSpec((1, own, width), lambda i, c, f: (i // per_span, 0, 0))
    whole = lambda shape: pl.BlockSpec(
        shape, lambda i, c, f: (0,) * len(shape), pipeline_mode=once
    )
    return pl.pallas_call(
        functools.partial(merge_kernel, n, ctx_count),
        grid_spec=pltpu.PrefetchScalarGridSpec(
            num_scalar_prefetch=2,
            grid=(count // tile,),
            in_specs=[whole((span, local))] * (2 * n)
            + [whole(pieces[0].shape)] * ctx_count
            + [row, whole((1, width)), whole(router_t.shape)],
            out_specs=[
                row,
                own_rows,
                pl.BlockSpec((router_t.shape[0], tile), lambda i, c, f: (0, i)),
                whole((n, local, width)),
                own_rows,
            ],
            scratch_shapes=[pltpu.VMEM((span, width), BF)],
        ),
        out_shape=[
            jax.ShapeDtypeStruct((count, width), BF),
            jax.ShapeDtypeStruct((count // span, own, width), F32),
            jax.ShapeDtypeStruct((router_t.shape[0], count), F32),
            jax.ShapeDtypeStruct((n, local, width), BF),
            jax.ShapeDtypeStruct((count // span, own, width), BF),
        ],
        compiler_params=pltpu.CompilerParams(vmem_limit_bytes=60 * MIB),
        cost_estimate=pl.CostEstimate(
            flops=2 * count * width * width, bytes_accessed=8 * count * width, transcendentals=0
        ),
        name="merge",
    )(c, shards, *got_a, *got_b, *pieces, rows, gain, router_t)


def project_back_kernel(seqs, dq_ref, *refs):
    pairs, refs = refs[:seqs], refs[seqs:]
    cos_ref, sin_ref, w_ref, h_ref, raw_ref, gn_ref, gain_ref = refs
    x = h_ref[...].astype(F32)
    inverse = lax.rsqrt(jnp.mean(x * x, axis=-1, keepdims=True) + EPSILON)
    cosine, sine = cos_ref[...], sin_ref[...]
    _, _, blocks, pr, local = pairs[0].shape
    raw_ref[0] = dq_ref[...]
    for b in range(blocks):
        for s in range(seqs):
            at = slice((b * seqs + s) * pr, (b * seqs + s + 1) * pr)
            raw_ref[2, at] = pairs[s][1, 0, b].astype(BF)
            for lo in range(0, local, HEAD_DIM):
                cols = slice(lo, lo + HEAD_DIM)
                part = pairs[s][0, 0, b, :, cols].astype(F32)
                part = part * cosine[at] - pltpu.roll(part, HEAD_DIM // 2, 1) * sine[at]
                raw_ref[1, at, cols] = part.astype(BF)
    gn = dot(raw_ref[0], w_ref[0], 1, 1)
    gn += dot(raw_ref[1], w_ref[1], 1, 1)
    gn += dot(raw_ref[2], w_ref[2], 1, 1)
    gn_ref[...] = gn.astype(BF)
    part = jnp.sum((gn * x * inverse).reshape(-1, 8, x.shape[1]), axis=0)

    @pl.when(pl.program_id(0) == 0)
    def _():
        gain_ref[...] = part

    @pl.when(pl.program_id(0) != 0)
    def _():
        gain_ref[...] += part


def project_back(dq, pairs, cosine, sine, weights, rows):
    count, width = rows.shape
    local = weights.shape[2]
    seqs = len(pairs)
    _, _, n, pr, _ = pairs[0].shape
    tile = 256
    blocks = tile // (seqs * pr)
    per_span = n // blocks
    row = lambda w: pl.BlockSpec((tile, w), lambda i: (i, 0))
    pair = pl.BlockSpec(
        (2, 1, blocks, pr, local), lambda i: (0, i // per_span, lax.rem(i, per_span), 0, 0)
    )
    return pl.pallas_call(
        functools.partial(project_back_kernel, seqs),
        grid=(count // tile,),
        in_specs=[row(local)]
        + [pair] * seqs
        + [
            row(HEAD_DIM),
            row(HEAD_DIM),
            pl.BlockSpec((3, width, local), lambda i: (0, 0, 0)),
            row(width),
        ],
        out_specs=[
            pl.BlockSpec((3, tile, local), lambda i: (0, i, 0)),
            row(width),
            pl.BlockSpec((8, width), lambda i: (0, 0)),
        ],
        out_shape=[
            jax.ShapeDtypeStruct((3, count, local), BF),
            jax.ShapeDtypeStruct((count, width), BF),
            jax.ShapeDtypeStruct((8, width), F32),
        ],
        compiler_params=pltpu.CompilerParams(vmem_limit_bytes=48 * MIB),
        cost_estimate=pl.CostEstimate(
            flops=6 * count * width * local, bytes_accessed=6 * count * width, transcendentals=0
        ),
        name="project_back",
    )(dq, *pairs, cosine, sine, weights, rows)


def spread(ref, rows):
    lead = ref.shape[:-2]
    if ref.shape[-2] % 16 == 0 or not lead:
        return [ref[...].reshape(rows, ref.shape[-1])]
    return [ref[index] for index in np.ndindex(*lead)]


def inner_kernel(expert_tiles, blocks, shard_ref, x_ref, *refs):
    c_refs, refs = refs[:blocks], refs[blocks:]
    mix_ref, ei_ref, si_ref, eo_ref, so_ref, d_ref, act_ref, dot_ref, c_all = refs
    k = pl.program_id(0)
    x_rows, c_rows = x_ref.shape[0], 256
    cut = c_refs[0].shape[2]

    @pl.when(k == 0)
    def _():
        for m in range(blocks):
            c_all[m * cut : (m + 1) * cut] = c_refs[m][0, 0]

    rows_in, rows_out = d_ref.shape[1], act_ref.shape[1]

    def finish(h_gate, h_up, u, scale):
        sig = 1.0 / (1.0 + jnp.exp(-h_gate))
        silu = h_gate * sig
        act = silu * h_up
        gu = u * scale
        d_gate = gu * h_up * sig * (1.0 + h_gate * (1.0 - sig))
        dots = jnp.sum(act * u, axis=0, keepdims=True)
        return (act * scale).astype(BF), d_gate.astype(BF), (gu * silu).astype(BF), dots

    def run(w_in, w_out, groups):
        size = rows_out // groups
        for lo in range(0, x_rows, c_rows):
            cols = slice(lo, lo + c_rows)
            xt, ct = x_ref[cols], c_all[cols]
            h = jnp.concatenate([dot(w, xt, 1, 1) for w in spread(w_in, rows_in)])
            u = jnp.concatenate([dot(w, ct, 1, 1) for w in spread(w_out, rows_out)])
            for g in range(groups):
                at = g * 2 * size
                act, dg, du, dots = finish(
                    h[at : at + size],
                    h[at + size : at + 2 * size],
                    u[g * size : (g + 1) * size],
                    mix_ref[0, g : g + 1, cols],
                )
                act_ref[0, g * size : (g + 1) * size, cols] = act
                d_ref[0, at : at + size, cols] = dg
                d_ref[0, at + size : at + 2 * size, cols] = du
                dot_ref[0, g : g + 1, cols] = dots

    @pl.when(k < expert_tiles)
    def _():
        run(ei_ref, eo_ref, 2)

    @pl.when(k >= expert_tiles)
    def _():
        run(si_ref, so_ref, 1)


def tile_specs(expert_in, shared_in, expert_out, shared_out, index, width):
    experts, _, f, _ = expert_in.shape
    last, share = experts // 2 - 1, 2 * f
    lo = lambda *i: jnp.minimum(index(*i), last)
    hi = lambda *i: jnp.maximum(index(*i) - last - 1, 0)
    return (
        pl.BlockSpec((2, 2, f, width), lambda *i: (lo(*i), 0, 0, 0)),
        pl.BlockSpec((2, share, width), lambda *i: (0, hi(*i), 0)),
        pl.BlockSpec((2, f, width), lambda *i: (lo(*i), 0, 0)),
        pl.BlockSpec((share, width), lambda *i: (hi(*i), 0)),
    )


def block_specs(n, cut, width):
    return [
        pl.BlockSpec(
            (1, 1, cut, width),
            lambda i, *p, t=t, k=k: (p[-1][t * n + k], t, 0, 0),
            pipeline_mode=pl.Buffered(1),
        )
        for t in range(2)
        for k in range(n)
    ]


def inner(shards, x, cot, mix, weights):
    rows, width = x.shape
    n, _, cut, _ = cot.shape
    expert_in, shared_in, expert_out, shared_out = weights
    f = expert_in.shape[2]
    tiles = expert_in.shape[0] // 2 + shared_out.shape[0] // (2 * f)
    whole = pl.BlockSpec((rows, width), lambda i, p: (0, 0), pipeline_mode=pl.Buffered(1))
    out = lambda r: pl.BlockSpec((1, r, rows), lambda i, p: (i, 0, 0))
    return pl.pallas_call(
        functools.partial(inner_kernel, expert_in.shape[0] // 2, 2 * n),
        grid_spec=pltpu.PrefetchScalarGridSpec(
            num_scalar_prefetch=1,
            grid=(tiles,),
            in_specs=[whole]
            + block_specs(n, cut, width)
            + [out(8), *tile_specs(*weights, lambda i, p: i, width)],
            out_specs=[out(4 * f), out(2 * f), out(8)],
            scratch_shapes=[pltpu.VMEM((rows, width), BF)],
        ),
        out_shape=[
            jax.ShapeDtypeStruct((tiles, 4 * f, rows), BF),
            jax.ShapeDtypeStruct((tiles, 2 * f, rows), BF),
            jax.ShapeDtypeStruct((tiles, 8, rows), F32),
        ],
        compiler_params=pltpu.CompilerParams(vmem_limit_bytes=62 * MIB),
        cost_estimate=pl.CostEstimate(
            flops=12 * f * rows * width * tiles,
            bytes_accessed=12 * f * width * tiles + 4 * rows * width,
            transcendentals=0,
        ),
        name="inner",
    )(shards, x, *[cot] * (2 * n), mix, *weights)


def outer_kernel(expert_tiles, shard_ref, d_ref, e_ref, s_ref, *refs):
    o_ref, acc = refs[-2:]
    k = pl.program_id(1)
    n, _, cut, _ = o_ref.shape

    @pl.when(k == 0)
    def _():
        acc[...] = jnp.zeros_like(acc)

    def run(w_ref):
        units = d_ref.shape[0] * d_ref.shape[1]
        hid = d_ref[...].reshape(units, d_ref.shape[2])
        at = 0
        for w in spread(w_ref, units):
            for lo in range(0, acc.shape[1], 512):
                acc[:, lo : lo + 512] += dot(
                    hid[at : at + w.shape[0]], w[:, lo : lo + 512], 0, 0
                )
            at += w.shape[0]

    @pl.when(k < expert_tiles)
    def _():
        run(e_ref)

    @pl.when(k >= expert_tiles)
    def _():
        run(s_ref)

    @pl.when(k == pl.num_programs(1) - 1)
    def _():
        first = pl.program_id(0) * n
        for m in range(n):
            to = m if shard_ref is None else shard_ref[first + m]
            o_ref[to, 0] = acc[m * cut : (m + 1) * cut].astype(BF)


def outer(shards, n, hid, expert, shared, *deps):
    tiles, units, tokens = hid.shape
    width, f = expert.shape[-1], expert.shape[-2]
    rows = tokens // 2
    if expert.ndim == 4:
        group, step = 1, 2
        e_shape, s_shape = (2, 2, f, width), (2, 2 * f, width)
    else:
        group, step = 2, 4
        e_shape, s_shape = (4, f, width), (4 * f, width)
    last = expert.shape[0] // step - 1
    lo = lambda k: jnp.minimum(k, last)
    hi = lambda k: jnp.maximum(k - last - 1, 0)
    if expert.ndim == 4:
        e_spec = pl.BlockSpec(e_shape, lambda t, k, *p: (lo(k), 0, 0, 0))
        s_spec = pl.BlockSpec(s_shape, lambda t, k, *p: (0, hi(k), 0))
    else:
        e_spec = pl.BlockSpec(e_shape, lambda t, k, *p: (lo(k), 0, 0))
        s_spec = pl.BlockSpec(s_shape, lambda t, k, *p: (hi(k), 0))
    return pl.pallas_call(
        functools.partial(outer_kernel, last + 1)
        if shards is not None
        else functools.partial(outer_kernel, last + 1, None),
        grid_spec=pltpu.PrefetchScalarGridSpec(
            num_scalar_prefetch=0 if shards is None else 1,
            grid=(2, tiles // group),
            in_specs=[pl.BlockSpec((group, units, rows), lambda t, k, *p: (k, 0, t)), e_spec, s_spec]
        + [pl.BlockSpec(memory_space=pl.ANY)] * len(deps),
            out_specs=pl.BlockSpec((n, 1, rows // n, width), lambda t, k, *p: (0, t, 0, 0)),
            scratch_shapes=[pltpu.VMEM((rows, width), F32)],
        ),
        out_shape=jax.ShapeDtypeStruct((n, 2, rows // n, width), BF),
        compiler_params=pltpu.CompilerParams(vmem_limit_bytes=58 * MIB),
        cost_estimate=pl.CostEstimate(
            flops=2 * tiles * units * tokens * width,
            bytes_accessed=2 * tiles * units * (tokens + 2 * width) + 2 * tokens * width,
            transcendentals=0,
        ),
        name="outer",
    )(*([] if shards is None else [shards]), hid, expert, shared, *deps)


def weight_kernel(blocks, core_ref, shard_ref, h_ref, *refs):
    o_ref = refs[-1]
    for lo in range(0, o_ref.shape[2], 512):
        cols = slice(lo, lo + 512)
        if blocks:
            other = jnp.concatenate([ref[0, 0, :, cols] for ref in refs[:blocks]])
        else:
            other = refs[0][:, cols]
        o_ref[0, :, cols] = dot(h_ref[0], other, 1, 0).astype(BF)


def weight_grad(core, shards, hid, other, base, stride, piece, pieces, *deps):
    _, units, tokens = hid.shape
    units = units // pieces
    width = other.shape[-1]
    if other.ndim == 4:
        specs = block_specs(other.shape[0], other.shape[2], width)
    else:
        specs = [
            pl.BlockSpec((tokens, width), lambda i, c, p: (0, 0), pipeline_mode=pl.Buffered(1))
        ]
    return pl.pallas_call(
        functools.partial(weight_kernel, len(specs) if other.ndim == 4 else 0),
        grid_spec=pltpu.PrefetchScalarGridSpec(
            num_scalar_prefetch=2,
            grid=(2,),
            in_specs=[
                pl.BlockSpec((1, units, tokens), lambda i, c, p: (base + stride * i, piece, 0)),
            ]
            + specs
            + [pl.BlockSpec(memory_space=pl.ANY)] * len(deps),
            out_specs=pl.BlockSpec(
                (1, units, width), lambda i, c, p: (lax.rem(i + c[0], 2), 0, 0)
            ),
        ),
        out_shape=jax.ShapeDtypeStruct((2, units, width), BF),
        compiler_params=pltpu.CompilerParams(vmem_limit_bytes=40 * MIB),
        cost_estimate=pl.CostEstimate(
            flops=4 * units * tokens * width,
            bytes_accessed=4 * units * (tokens + width) + 2 * tokens * width,
            transcendentals=0,
        ),
        name="weight_grad",
    )(core, shards, hid, *[other] * len(specs), *deps)


def finish_kernel(core_ref, *refs):
    o_ref = refs[-1]
    which = pl.program_id(0) * pl.num_programs(1) + pl.program_id(1)
    for m, ref in enumerate(refs[:-1]):

        @pl.when(which == m)
        def _(ref=ref):
            o_ref[...] = ref[...].astype(F32).reshape(o_ref.shape)


def finish(core, kept, got, gated):
    count = len(kept)
    rows, width = kept[0].shape
    tile = rows // 2 if rows % 32 == 0 else rows
    steps = rows // tile
    at = lambda m: lambda h, j, r, c: (
        jnp.where(h * count + j == m, r, jnp.where(h * count + j < m, 0, steps - 1)),
        0,
    )
    if gated:
        shape = (count, 2, rows, width)
        place = lambda h, j, r, c: (j, lax.rem(h + c[0], 2), r, 0)
    else:
        shape = (2, count, rows, width)
        place = lambda h, j, r, c: (lax.rem(h + c[0], 2), j, r, 0)
    return pl.pallas_call(
        finish_kernel,
        grid_spec=pltpu.PrefetchScalarGridSpec(
            num_scalar_prefetch=1,
            grid=(2, count, steps),
            in_specs=[pl.BlockSpec((tile, width), at(m)) for m in range(2 * count)],
            out_specs=pl.BlockSpec((1, 1, tile, width), place),
        ),
        out_shape=jax.ShapeDtypeStruct(shape, F32),
        compiler_params=pltpu.CompilerParams(vmem_limit_bytes=40 * MIB),
        cost_estimate=pl.CostEstimate(
            flops=0, bytes_accessed=12 * count * rows * width, transcendentals=0
        ),
        name="finish",
    )(core, *kept, *got)


class Ring:
    def __init__(self, count):
        self.count = count
        self.order = ring_order(count)
        self.place = np.argsort(np.array(self.order))

    def shift(self, value, by):
        n = self.count
        pairs = [(self.order[i], self.order[(i + by) % n]) for i in range(n)]
        return lax.ppermute(value, "fsdp", pairs)

    def gather(self, ahead, behind):
        a, b = [ahead], [behind]
        for _ in range(self.count - 1):
            a.append(self.shift(a[-1], 1))
            b.append(self.shift(b[-1], -1))
        return a, b

    def scatter(self, ahead, behind, work=()):
        n = self.count
        a, b = ahead(1), behind(1)
        held = []
        for k in range(2, n + 1):
            kind = BF if k < n else F32
            a = (self.shift(a, 1).astype(F32) + ahead(k % n).astype(F32)).astype(kind)
            b = (self.shift(b, -1).astype(F32) + behind(k % n).astype(F32)).astype(kind)
            if held:
                a, b = after(a, *held), after(b, *held)
            held = work(k, a, b) if work else []
        return a, b, held


def ctx_pairs(ctx_count, lanes, core):
    half = ctx_count // 2
    return [(x * 2 + k, ((x + lanes) % half) * 2 + (k ^ core)) for x in range(half) for k in range(2)]


def ctx_gather(value, ctx_count):
    got = []
    for lanes in range(ctx_count // 2):
        mine = value if lanes == 0 else lax.ppermute(value, "ctx", ctx_pairs(ctx_count, lanes, 0))
        got.append(mine)
        got.append(lax.ppermute(mine, "ctx", ctx_pairs(ctx_count, 0, 1)))
    return got


def ctx_scatter(parts, ctx_count):
    half = ctx_count // 2
    total = None
    for lanes in reversed(range(half)):
        other = lax.ppermute(parts[2 * lanes + 1], "ctx", ctx_pairs(ctx_count, 0, 1))
        s = parts[2 * lanes].astype(F32) + other.astype(F32)
        if lanes:
            s = lax.ppermute(s.astype(BF), "ctx", ctx_pairs(ctx_count, -lanes % half, 0)).astype(F32)
        total = s if total is None else total + s
    return total


class Sum:
    def __init__(self, value):
        self.value = value

    def reduce(self):
        flip = ctx_pairs(4, 0, 1)
        keep, send = self.value[0], self.value[1]
        self.part = (keep.astype(F32) + lax.ppermute(send, "ctx", flip).astype(F32)).astype(BF)
        return self.part

    def cross(self, *ties):
        part = after(self.part, *ties) if ties else self.part
        self.got = lax.ppermute(part, "ctx", ctx_pairs(4, 1, 0))
        return self.got

    def finish(self, *ties):
        got = after(self.got, *ties) if ties else self.got
        t = (self.part.astype(F32) + got.astype(F32)).astype(BF)
        return t, lax.ppermute(t, "ctx", ctx_pairs(4, 0, 1))


def kept_table(route_rows, keys, experts, capacity):
    index = jnp.arange(keys.shape[0], dtype=jnp.int32)
    before = (keys[None, :] < keys[:, None]) | (
        (keys[None, :] == keys[:, None]) & (index[None, :] < index[:, None])
    )
    named = jnp.any(
        route_rows[None, :, :] == jnp.arange(experts, dtype=jnp.int32)[:, None, None], axis=2
    )
    ahead = dot(named.astype(BF), before.astype(BF), 1, 1)
    return (named & (ahead < capacity)).astype(BF)


def per_device(
    hidden_in,
    cotangent,
    routes,
    priority,
    gain_attn,
    attention_input_weights,
    attention_output_weights,
    gain_ffn,
    router,
    shared_gate,
    shared_in,
    shared_out,
    expert_in,
    expert_out,
):
    n = lax.axis_size("fsdp")
    ctx_count = lax.axis_size("ctx")
    c = lax.axis_index("ctx")
    core = lax.rem(c, 2)
    ring = Ring(n)
    place = jnp.asarray(ring.place, jnp.int32)[lax.axis_index("fsdp")]
    seqs, _, _, pr, width = hidden_in.shape
    span = pr * n
    local = attention_input_weights.shape[2]
    experts = expert_in.shape[0]
    top = routes.shape[-1]
    own_rows = seqs * 2 * pr
    tokens = own_rows * n
    capacity = 5 * own_rows * top // (4 * experts)
    slices = width // n

    cut = seqs * pr
    hidden = jnp.transpose(hidden_in[:, :, 0], (1, 0, 2, 3)).reshape(2, cut, width)

    def as_rows(value):
        value = value.reshape(-1)
        return jnp.pad(value, (0, 8 * width - value.size)).reshape(8, width)

    small = jnp.concatenate([gain_attn[None], gain_ffn[None], shared_gate[None], router.T])
    small_count = small.shape[0]
    got_a, got_b = ring.gather(jnp.concatenate([hidden[0], as_rows(small)]), hidden[1])
    last = got_a[-1], got_b[-1]
    places = jnp.asarray(ring.place, jnp.int32)
    order = jnp.asarray(ring.order, jnp.int32)
    steps = jnp.arange(n, dtype=jnp.int32)
    place = after(place, got_a[2])
    by_shard = (place - places) % n
    shards = jnp.stack([order[(place - steps) % n], order[(place + steps) % n]])
    offset = shards[:, :, None] * pr + jnp.arange(pr, dtype=jnp.int32)
    c_later = after(c, got_a[3])
    start = jnp.stack([c_later, 2 * ctx_count - 1 - c_later]) * span
    positions = start[:, None, None] + offset
    flags = (offset // BLOCK).astype(F32).reshape(2, span)
    flag_col, flag_row = flags[:, :, None], flags[:, None, :]
    halves = jnp.arange(HEAD_DIM, dtype=jnp.int32) % (HEAD_DIM // 2)
    frequency = ROPE_BASE ** (-2.0 * halves.astype(F32) / HEAD_DIM)
    angles = positions.astype(F32)[..., None] * frequency
    sign = jnp.where(jnp.arange(HEAD_DIM) < HEAD_DIM // 2, -1.0, 1.0)
    by_seq = (2, n, seqs, pr, HEAD_DIM)
    cosine = jnp.broadcast_to(jnp.cos(angles)[:, :, None], by_seq)
    sine = jnp.broadcast_to((jnp.sin(angles) * sign)[:, :, None], by_seq)
    flat_cos, flat_sin = cosine.reshape(tokens, HEAD_DIM), sine.reshape(tokens, HEAD_DIM)

    shard_list = shards.reshape(-1)
    c_arr = c.reshape(1).astype(jnp.int32)
    core_arr = core.reshape(1).astype(jnp.int32)
    smalls = jnp.stack([g[cut:].reshape(-1)[: small.size] for g in got_a])
    smalls = smalls.reshape(n, small_count, slices)
    smalls = jnp.take(smalls, by_shard, axis=0)
    smalls = jnp.transpose(smalls, (1, 0, 2)).reshape(small_count, width)
    all_rows = jnp.concatenate([g[:cut] for g in got_a] + got_b)
    gain_one, gain_two = smalls[0:1].astype(F32), smalls[1:2].astype(F32)
    logit_rows = jnp.concatenate(
        [smalls[3:], smalls[2:3], jnp.zeros((16 - experts - 1, width), BF)]
    )

    share = local // ctx_count
    mine = lax.dynamic_slice_in_dim(attention_output_weights, c * share, share, 0)
    out_piece = lax.all_gather(mine, "fsdp", axis=0)
    out_pieces = ctx_gather(out_piece, ctx_count)
    cot = jnp.transpose(cotangent[:, :, 0], (1, 0, 2, 3)).reshape(2, cut, width)
    cot_all = lax.all_gather(after(cot, got_a[n - 3]), "fsdp", axis=0)
    routes_in, priority_in = after(routes, got_a[5]), after(priority, got_a[5])
    kept_own = kept_table(
        routes_in.reshape(own_rows, top), priority_in.reshape(own_rows), experts, capacity
    )
    kept_fill = -(-kept_own.size // local) % 8
    kept_rows = jnp.pad(kept_own.reshape(-1, local), ((0, kept_fill and 8 - kept_fill), (0, 0)))

    normed_one, query, kv_own = project(
        all_rows, gain_one, attention_input_weights, flat_cos, flat_sin, seqs, n
    )
    query = query.reshape(2, n, seqs, pr, local)
    kvs = []
    for s in range(seqs):
        pieces = ctx_gather(kv_own[s], ctx_count)
        kvs.append(jnp.stack(pieces).reshape(ctx_count, 2, 2, span, local))

    mixed, log_sums = None, []
    for s in range(seqs):
        mixed, lse = attend(c_arr, query, kvs[s], s, flag_col, flag_row, mixed)
        log_sums.append(lse)
    sent = mixed.reshape(2, tokens // 2, local)
    got_a, got_b = ring.gather(jnp.concatenate([sent[0], kept_rows]), sent[1])
    kept = [
        g[tokens // 2 :].reshape(-1)[: kept_own.size].reshape(experts, seqs, 2, pr) for g in got_a
    ]
    kept = jnp.stack(
        [
            jnp.stack([g[:, :, 0] for g in kept], axis=1),
            jnp.stack([kept[(n - k) % n][:, :, 1] for k in range(n)], axis=1),
        ],
        axis=1,
    )
    kept = kept.reshape(experts, tokens).astype(F32)
    x, resid, logit, out_full, mixed_own = merge(
        c_arr, shard_list, got_a, got_b, out_pieces, all_rows, gain_two, logit_rows
    )
    out_full = out_full.reshape(width, width)
    resid = resid.reshape(own_rows, width)

    top_logit = jnp.max(logit[:experts], axis=0, keepdims=True)
    raised = jnp.exp(logit[:experts] - top_logit)
    gates = raised / jnp.sum(raised, axis=0, keepdims=True)
    weight_s = jax.nn.sigmoid(logit[experts : experts + 1])
    small_tiles = shared_out.shape[0] // (2 * expert_in.shape[2])
    mix = jnp.concatenate(
        [
            jnp.pad((gates * kept).reshape(experts // 2, 2, tokens), ((0, 0), (0, 6), (0, 0))),
            jnp.broadcast_to(jnp.pad(weight_s, ((0, 7), (0, 0)))[None], (small_tiles, 8, tokens)),
        ]
    )
    d_buf, act_buf, dots = inner(
        shard_list, x, cot_all, mix, (expert_in, shared_in, expert_out, shared_out)
    )
    split = lambda value: value.reshape(2, n, cut, width)
    dots_e = dots[: experts // 2, :2].reshape(experts, tokens) * kept
    dots_s = jnp.sum(dots[experts // 2 :, 0], axis=0, keepdims=True)
    dots = jnp.concatenate([dots_e, dots_s, jnp.zeros((7, tokens), F32)])
    dots = dots.reshape(16, 2, n, cut)
    dots = jnp.stack(
        [jnp.take(dots[:, 0], by_shard, axis=1), jnp.take(dots[:, 1], -by_shard % n, axis=1)],
        axis=2,
    )
    dots = jnp.transpose(dots, (1, 0, 2, 3)).reshape(n, 16, own_rows)
    dot_own = lax.psum_scatter(dots, "fsdp", scatter_dimension=0, tiled=True)[0]

    f = expert_in.shape[2]
    quarter = experts // 4
    halves = small_tiles // 2
    four = ctx_count == 4
    spots = [(j, quarter) for j in range(quarter)] + [
        (experts // 2 + j, halves) for j in range(halves)
    ]
    sums = {}

    def weight_piece(key, *ties):
        name, base, piece = key
        buf, other = (d_buf, x) if name == "in" else (act_buf, cot_all)
        sums[key] = Sum(
            weight_grad(
                core_arr,
                shard_list,
                buf,
                other,
                base,
                dict(spots)[base],
                piece,
                2 if name == "in" else 1,
                *ties,
            )
        )
        return sums[key].value

    late = [("out", base, 0) for base, _ in spots]
    queue = [("in", base, piece) for base, _ in spots for piece in (0, 1)]
    flown = []

    def fly(key):
        if four:
            sums[key].reduce()
            flown.append(sums[key].cross(*flown[-2:-1]))
            return [flown[-1]]
        return []

    early = []
    for key in late[:2]:
        early.append(weight_piece(key))
    early_got = [fly(key) for key in late[:2]]
    if four:
        early = [sums[key].part for key in late[:2]]
    grad_in = outer(None, n, d_buf, expert_in, shared_in, *early)

    def beside(k, a, b):
        held = []
        if k - 2 < len(queue):
            held.append(weight_piece(queue[k - 2], a, b))
        if four and 0 <= k - 3 < len(queue):
            held.append(sums[queue[k - 3]].reduce())
            flown.append(sums[queue[k - 3]].cross(*flown[-2:-1]))
        if k in (3, 5):
            held += early_got[(k - 3) // 2]
        if k == n - 1 and four:
            held.append(sums[queue[0]].got)
        return held

    gi_a, gi_b, _ = ring.scatter(lambda k: grad_in[k, 0], lambda k: grad_in[k, 1], beside)
    for key in queue[n - 1 :]:
        weight_piece(key, gi_a, gi_b)
    if four:
        for key in queue[n - 2 :]:
            sums[key].reduce()
            flown.append(sums[key].cross(*flown[-2:-1]))
    got_in = [sums[key].got for key in queue] if four else []

    def norm_back(grad, value, gain):
        inverse = lax.rsqrt(jnp.mean(value * value, axis=-1, keepdims=True) + EPSILON)
        scaled = grad * gain
        return inverse * (
            scaled - value * inverse * inverse * jnp.mean(scaled * value, axis=-1, keepdims=True)
        ), inverse

    own_of = lambda value: value.reshape(-1, 2, n, cut)[:, :, 0].reshape(-1, own_rows)
    gates_own, weight_own = own_of(gates), own_of(weight_s)
    x_own = split(x)[:, 0].reshape(own_rows, width)
    d_gates = dot_own[:experts]
    d_logit = (
        gates_own * (d_gates - jnp.sum(gates_own * d_gates, axis=0, keepdims=True))
    ).astype(BF)
    d_gate_s = dot_own[experts : experts + 1] * weight_own * (1.0 - weight_own)
    d_rows = jnp.concatenate([d_gate_s, d_logit.astype(F32)])
    grad_n2 = jnp.concatenate([gi_a, gi_b])
    grad_n2 = grad_n2 + jnp.einsum("er,ed->rd", d_rows, smalls[2:].astype(F32), precision=EXACT)
    grad_small = jnp.einsum("er,rd->ed", d_rows, x_own.astype(F32), precision=EXACT)
    back, inverse_two = norm_back(grad_n2, resid, gain_two)
    grad_gain_two = jnp.sum(grad_n2 * resid * inverse_two, axis=0, keepdims=True)
    grad_mid = cot.reshape(own_rows, width).astype(F32) + back
    branch = grad_mid.astype(BF)

    grad_mixed = dot(branch, out_full, 1, 1).astype(BF)
    grad_mixed = jnp.take(grad_mixed.reshape(own_rows, n, local), by_shard, axis=1)
    grad_mixed = jnp.transpose(grad_mixed, (1, 0, 2))
    out_part = outer(shard_list, n, act_buf, expert_out, shared_out, grad_mixed, *got_in[1:2])
    moved = lax.all_to_all(
        grad_mixed, "fsdp", split_axis=0, concat_axis=0, tiled=True
    ).reshape(n, 2, cut, local)
    d_o = jnp.concatenate(
        [jnp.take(moved[:, 0], shards[0], axis=0), jnp.take(moved[:, 1], shards[1], axis=0)]
    ).reshape(2, n, seqs, pr, local)
    d_o = after(d_o, out_part)

    in_place = lambda value: jnp.transpose(
        value.reshape(2, seqs, pr, width), (1, 0, 2, 3)
    ).reshape(hidden_in.shape)
    out_own = lax.psum_scatter(out_part, "fsdp", scatter_dimension=0, tiled=True)

    d_q, pairs = None, []
    for s in range(seqs):
        d_q, pair = attend_back(
            c_arr,
            query,
            kvs[s],
            d_o,
            mixed,
            log_sums[s],
            s,
            cosine,
            sine,
            flag_col,
            flag_row,
            d_q,
            *got_in[2 + s : 3 + s],
        )
        pair = ctx_scatter([pair[j] for j in range(ctx_count)], ctx_count)
        pairs.append(pair.astype(BF).reshape(2, 2, n, pr, local))
    d_q = after(d_q, out_own, *got_in[4:5])

    grad_out_own = dot(mixed_own.reshape(own_rows, width), branch, 0, 0).astype(BF)
    if four:
        flip, cross = ctx_pairs(4, 0, 1), ctx_pairs(4, 1, 0)
        lane = c // 2
        pick = lambda value, i, axis: lax.dynamic_index_in_dim(value, i, axis, keepdims=False)
        by_core = grad_out_own.reshape(n, 2, 2, share, width)
        part = pick(by_core, core, 2).astype(F32)
        part = part + lax.ppermute(pick(by_core, 1 - core, 2), "ctx", flip).astype(F32)
        part = part.astype(BF)
        quart_got = lax.ppermute(after(pick(part, 1 - lane, 1), *pairs), "ctx", cross)
    else:
        quart_got = lax.psum(grad_out_own, "ctx").reshape(n, local, width)

    raw, grad_n1, gain_part = project_back(
        d_q.reshape(tokens, local), pairs, flat_cos, flat_sin, attention_input_weights, all_rows
    )
    quart_got = after(quart_got, raw)
    quart = (pick(part, lane, 1).astype(F32) + quart_got.astype(F32)).astype(BF) if four else quart_got
    quart = jnp.take(quart, by_shard, axis=0)
    own_quart = lax.psum_scatter(quart, "fsdp", scatter_dimension=0, tiled=True)[0]

    grad_n1 = split(grad_n1)
    grad_gain_one = jnp.sum(gain_part, axis=0, keepdims=True)
    smalls_back = jnp.concatenate(
        [grad_gain_one, grad_gain_two, grad_small, jnp.zeros((16 - small_count, width), F32)]
    )
    smalls_back = jnp.transpose(smalls_back.reshape(16, n, slices), (1, 0, 2))
    small_own = lax.psum_scatter(smalls_back, "fsdp", scatter_dimension=0, tiled=True)[0]

    def beside_last(k, a, b):
        held = []
        if k == 2:
            held += [weight_piece(key, a, b) for key in late[2:]]
        if k == 3 and four:
            held += got_in[5:6]
            for key in late[2:]:
                sums[key].reduce()
                sums[key].cross(quart_got)
        if k == 5 and four:
            held.append(quart_got)
        if k == n - 1 and four:
            held += [sums[key].got for key in late[2:]]
        return held

    gn_a, gn_b, _ = ring.scatter(lambda k: grad_n1[0, k], lambda k: grad_n1[1, k], beside_last)
    back_one, _ = norm_back(
        jnp.concatenate([gn_a, gn_b]), hidden.reshape(own_rows, width).astype(F32), gain_one
    )
    grad_hidden = in_place((grad_mid + back_one).astype(BF))
    out_own = after(out_own, gn_a, gn_b).reshape(own_rows, width).astype(F32)
    layer_out = in_place((resid + out_own).astype(BF))
    small_own = after(small_own, gn_a, gn_b)
    if ctx_count == 4:
        small_own = small_own + lax.ppermute(small_own, "ctx", ctx_pairs(4, 0, 1))
        small_own = small_own + lax.ppermute(small_own, "ctx", ctx_pairs(4, 1, 0))
    else:
        small_own = lax.psum(small_own, "ctx")

    grad_attn_in = jnp.einsum("nd,jne->dje", normed_one, raw, preferred_element_type=F32)

    own_quart = after(own_quart, gn_a, gn_b)
    if ctx_count == 4:
        t = own_quart
        o = lax.ppermute(t, "ctx", cross)
        t = jnp.stack([jnp.where(lane == 0, t, o), jnp.where(lane == 0, o, t)])
        o = lax.ppermute(t, "ctx", flip)
        total_attn_out = jnp.stack(
            [jnp.where(core == 0, t, o), jnp.where(core == 0, o, t)], axis=1
        ).astype(F32)
    else:
        total_attn_out = own_quart.astype(F32)

    lo = range(quarter)
    hi = range(experts // 2, experts // 2 + halves)
    if four:
        done = {
            key: value.finish(*([raw] if key in queue[:4] else [gn_a, gn_b]))
            for key, value in sums.items()
        }

        def finished(keys, gated):
            kept_halves, got_halves = zip(*[done[key] for key in keys])
            return finish(core_arr, kept_halves, got_halves, gated)

        def halved(value):
            keep = lax.dynamic_index_in_dim(value, core, 0, keepdims=False)
            send = lax.dynamic_index_in_dim(value, 1 - core, 0, keepdims=False)
            one = Sum((keep.astype(BF), send.astype(BF)))
            one.reduce()
            one.cross(*([sums[key].got for key in late[2:]]))
            t, o = one.finish(gn_a, gn_b)
            return jnp.stack([jnp.where(core == 0, t, o), jnp.where(core == 0, o, t)]).astype(F32)

        total_expert_in = finished([("in", j, p) for j in lo for p in (0, 1)], False)
        total_expert_out = finished([("out", j, 0) for j in lo], False)
        total_shared_in = finished([("in", j, p) for j in hi for p in (0, 1)], True)
        total_shared_out = finished([("out", j, 0) for j in hi], False)
        total_attn_in = halved(grad_attn_in.reshape(2, width // 2, 3, local))
    else:
        first = core == 0

        def summed(keys, axis):
            values = [
                jnp.where(first, sums[key].value, jnp.flip(sums[key].value, axis=0))
                for key in keys
            ]
            return lax.psum(jnp.stack(values, axis=axis), "ctx").astype(F32)

        total_expert_in = summed([("in", j, p) for j in lo for p in (0, 1)], 1)
        total_expert_out = summed([("out", j, 0) for j in lo], 1)
        total_shared_in = summed([("in", j, p) for j in hi for p in (0, 1)], 0)
        total_shared_out = summed([("out", j, 0) for j in hi], 1)
        total_attn_in = lax.psum(grad_attn_in.astype(BF), "ctx").astype(F32)

    return (
        layer_out,
        grad_hidden,
        small_own[0],
        jnp.transpose(total_attn_in.reshape(width, 3, local), (1, 0, 2)),
        total_attn_out.reshape(local, width),
        small_own[1],
        small_own[3:small_count].T,
        small_own[2],
        total_shared_in.reshape(shared_in.shape),
        total_shared_out.reshape(shared_out.shape),
        total_expert_in.reshape(expert_in.shape),
        total_expert_out.reshape(expert_out.shape),
    )


def solution(mesh):
    rows = P(None, None, "ctx", "fsdp", None)
    return jax.shard_map(
        per_device,
        mesh=mesh,
        in_specs=(
            rows,
            rows,
            rows,
            P(None, None, "ctx", "fsdp"),
            P("fsdp"),
            P(None, None, "fsdp"),
            P("fsdp", None),
            P("fsdp"),
            P("fsdp", None),
            P("fsdp"),
            P(None, "fsdp", None),
            P("fsdp", None),
            P(None, None, "fsdp", None),
            P(None, "fsdp", None),
        ),
        out_specs=(
            rows,
            rows,
            P("fsdp"),
            P(None, None, "fsdp"),
            P("fsdp", None),
            P("fsdp"),
            P("fsdp", None),
            P("fsdp"),
            P(None, "fsdp", None),
            P("fsdp", None),
            P(None, None, "fsdp", None),
            P(None, "fsdp", None),
        ),
        check_vma=False,
    )
```

```python
import functools

import jax
import jax.numpy as jnp
import numpy as np
from jax import lax
from jax.experimental import pallas as pl
from jax.experimental.pallas import tpu as pltpu
from jax.sharding import PartitionSpec as P

HEAD_DIM = 128
BLOCK = 256
EPSILON = 1e-06
ROPE_BASE = 1000000.0
LOG2E = 1.4426950408889634
EXACT = lax.Precision.HIGHEST
BF = jnp.bfloat16
F32 = jnp.float32
MIB = 1 << 20


def ring_order(count):
    if count == 8:
        return [0, 2, 4, 6, 7, 5, 3, 1]
    side = int(round(count**0.5))
    if side * side != count:
        return list(range(count))
    order = []
    for row in range(side):
        line = [row * side + col for col in range(side)]
        order += line if row % 2 == 0 else line[::-1]
    return order


def after(value, *others):
    return lax.optimization_barrier((value, *others))[0]


def dot(a, b, ca, cb):
    return lax.dot_general(a, b, (((ca,), (cb,)), ((), ())), preferred_element_type=F32)


def project_kernel(h_ref, gain_ref, w_ref, cos_ref, sin_ref, n_ref, q_ref, kv_ref):
    x = h_ref[...].astype(F32)
    inverse = lax.rsqrt(jnp.mean(x * x, axis=-1, keepdims=True) + EPSILON)
    normed = (x * inverse * gain_ref[...]).astype(BF)
    n_ref[...] = normed
    cosine, sine = cos_ref[...], sin_ref[...]
    seqs, _, _, blocks, pr, _ = kv_ref.shape
    for j in range(3):
        y = dot(normed, w_ref[j], 1, 0)
        for lo in range(0, y.shape[1], HEAD_DIM):
            cols = slice(lo, lo + HEAD_DIM)
            part = y[:, cols]
            if j < 2:
                part = part * cosine + pltpu.roll(part, HEAD_DIM // 2, 1) * sine
            part = part.astype(BF)
            if j == 0:
                q_ref[:, cols] = part
            else:
                for b in range(blocks):
                    for s in range(seqs):
                        at = (b * seqs + s) * pr
                        kv_ref[s, j - 1, 0, b, :, cols] = part[at : at + pr]


def project(rows, gain, weights, cosine, sine, seqs, n):
    count, width = rows.shape
    local = weights.shape[2]
    tile = 256
    pr = count // (2 * n * seqs)
    blocks = tile // (seqs * pr)
    per_span = n // blocks
    row = lambda w: pl.BlockSpec((tile, w), lambda i: (i, 0))
    return pl.pallas_call(
        project_kernel,
        grid=(count // tile,),
        in_specs=[
            row(width),
            pl.BlockSpec((1, width), lambda i: (0, 0)),
            pl.BlockSpec((3, width, local), lambda i: (0, 0, 0)),
            row(HEAD_DIM),
            row(HEAD_DIM),
        ],
        out_specs=[
            row(width),
            row(local),
            pl.BlockSpec(
                (seqs, 2, 1, blocks, pr, local),
                lambda i: (0, 0, i // per_span, lax.rem(i, per_span), 0, 0),
            ),
        ],
        out_shape=[
            jax.ShapeDtypeStruct((count, width), BF),
            jax.ShapeDtypeStruct((count, local), BF),
            jax.ShapeDtypeStruct((seqs, 2, 2, n, pr, local), BF),
        ],
        compiler_params=pltpu.CompilerParams(vmem_limit_bytes=40 * MIB),
        cost_estimate=pl.CostEstimate(
            flops=6 * count * width * local, bytes_accessed=4 * count * width, transcendentals=0
        ),
        name="project",
    )(rows, gain, weights, cosine, sine)


def relative(c, other, ctx_count):
    lanes = ctx_count // 2
    apart = lax.rem(c // 2 - other // 2 + lanes, lanes)
    return apart * 2 + lax.rem(c + other, 2)


def attend_kernel(ctx_count, c_ref, q_ref, k_ref, v_ref, fc_ref, fr_ref, *refs):
    o_ref, lse_ref = refs[-2:]
    c = c_ref[0]
    kind = pl.program_id(1)
    q = q_ref[...].reshape(k_ref.shape[3:])
    scale = HEAD_DIM**-0.5 * LOG2E

    def diag():
        s = dot(q, k_ref[0, 0, kind], 1, 1) * scale
        s = jnp.where(fr_ref[0] <= fc_ref[0], s, -1e30)
        m = jnp.max(s, axis=-1, keepdims=True)
        p = jnp.exp2(s - m)
        return m, jnp.sum(p, axis=-1, keepdims=True), dot(p.astype(BF), v_ref[0, 0, kind], 1, 0)

    def step(other, pp, state):
        m, l, acc = state
        j = relative(c, other, ctx_count)
        s = dot(q, k_ref[j, 0, pp], 1, 1) * scale
        m_new = jnp.maximum(m, jnp.max(s, axis=-1, keepdims=True))
        p = jnp.exp2(s - m_new)
        a = jnp.exp2(m - m_new)
        return (
            m_new,
            l * a + jnp.sum(p, axis=-1, keepdims=True),
            acc * a + dot(p.astype(BF), v_ref[j, 0, pp], 1, 0),
        )

    state = diag()
    state = lax.fori_loop(
        0, jnp.where(kind == 0, c, ctx_count), lambda i, st: step(i, 0, st), state
    )
    state = lax.fori_loop(
        jnp.where(kind == 0, ctx_count, c + 1), ctx_count, lambda i, st: step(i, 1, st), state
    )
    m, l, acc = state
    o_ref[...] = (acc / l).astype(BF).reshape(o_ref.shape)
    lse = jnp.broadcast_to(m + jnp.log2(l), acc.shape)
    lse_ref[0, 0] = jnp.transpose(lse)[:8]


def attend(c, q, kv, seq, flag_col, flag_row, out):
    ctx_count, _, _, span, local = kv.shape
    heads = local // HEAD_DIM
    _, n, _, pr, _ = q.shape
    block = (ctx_count, 1, 2, span, HEAD_DIM)
    ks = pl.BlockSpec(block, lambda h, t, c: (0, 0, 0, 0, h))
    vs = pl.BlockSpec(block, lambda h, t, c: (0, 1, 0, 0, h))
    qs = pl.BlockSpec((1, n, 1, pr, HEAD_DIM), lambda h, t, c: (t, 0, seq, 0, h))
    held = [] if out is None else [out]
    return pl.pallas_call(
        functools.partial(attend_kernel, ctx_count),
        grid_spec=pltpu.PrefetchScalarGridSpec(
            num_scalar_prefetch=1,
            grid=(heads, 2),
            in_specs=[
                qs,
                ks,
                vs,
                pl.BlockSpec((1, span, 1), lambda h, t, c: (t, 0, 0)),
                pl.BlockSpec((1, 1, span), lambda h, t, c: (t, 0, 0)),
            ]
            + [pl.BlockSpec(memory_space=pl.ANY)] * len(held),
            out_specs=[qs, pl.BlockSpec((1, 1, 8, span), lambda h, t, c: (h, t, 0, 0))],
        ),
        out_shape=[
            jax.ShapeDtypeStruct(q.shape, BF),
            jax.ShapeDtypeStruct((heads, 2, 8, span), F32),
        ],
        input_output_aliases={6: 0} if held else {},
        compiler_params=pltpu.CompilerParams(vmem_limit_bytes=48 * MIB),
        cost_estimate=pl.CostEstimate(
            flops=heads * 9 * 8 * span * span * HEAD_DIM, bytes_accessed=8 * MIB, transcendentals=0
        ),
        name="attend",
    )(c, q, kv, kv, flag_col, flag_row, *held)


def attend_back_kernel(
    ctx_count,
    c_ref,
    q_ref,
    k_ref,
    v_ref,
    do_ref,
    o_ref,
    lse_ref,
    cos_ref,
    sin_ref,
    fc_ref,
    fr_ref,
    *refs,
):
    dq_ref, dkv_ref, dk_acc, dv_acc, dq_acc = refs[-5:]
    flat = (k_ref.shape[3], k_ref.shape[4])
    c = c_ref[0]
    root = HEAD_DIM**-0.5
    dk_acc[...] = jnp.zeros_like(dk_acc)
    dv_acc[...] = jnp.zeros_like(dv_acc)
    for kind in range(2):
        q, do = q_ref[kind].reshape(flat), do_ref[kind].reshape(flat)
        product = do.astype(F32) * o_ref[kind].reshape(flat).astype(F32)
        delta = jnp.sum(jnp.transpose(product), axis=0, keepdims=True)
        lse = lse_ref[0, kind, 0:1]
        dq_acc[...] = jnp.zeros_like(dq_acc)

        def step(j, pp, masked, q=q, do=do, delta=delta, lse=lse, kind=kind):
            k, v = k_ref[j, 0, pp], v_ref[j, 0, pp]
            s = dot(k, q, 1, 1) * (root * LOG2E)
            if masked:
                s = jnp.where(fc_ref[kind] <= fr_ref[kind], s, -1e30)
            p = jnp.exp2(s - lse)
            dp = dot(v, do, 1, 1)
            ds = (p * (dp - delta)).astype(BF)
            dv_acc[j, pp] += dot(p.astype(BF), do, 1, 0)
            dk_acc[j, pp] += dot(ds, q, 1, 0)
            dq_acc[...] += dot(ds, k, 0, 0)

        step(0, kind, True)

        def plain(i, carry, pp):
            step(relative(c, i, ctx_count), pp, False)
            return carry

        if kind == 0:
            lax.fori_loop(0, c, functools.partial(plain, pp=0), 0)
        else:
            lax.fori_loop(0, ctx_count, functools.partial(plain, pp=0), 0)
            lax.fori_loop(c + 1, ctx_count, functools.partial(plain, pp=1), 0)
        dq = dq_acc[...] * root
        cosine, sine = cos_ref[kind].reshape(flat), sin_ref[kind].reshape(flat)
        dq = dq * cosine - pltpu.roll(dq, HEAD_DIM // 2, 1) * sine
        dq_ref[kind] = dq.astype(BF).reshape(dq_ref.shape[1:])
    dkv_ref[:, 0] = (dk_acc[...] * root).astype(BF)
    dkv_ref[:, 1] = dv_acc[...].astype(BF)


def attend_back(c, q, kv, do, o, lse, seq, cosine, sine, flag_col, flag_row, out, *deps):
    ctx_count, _, _, span, local = kv.shape
    heads = local // HEAD_DIM
    _, n, _, pr, _ = q.shape
    block = (ctx_count, 1, 2, span, HEAD_DIM)
    ks = pl.BlockSpec(block, lambda h, c: (0, 0, 0, 0, h))
    vs = pl.BlockSpec(block, lambda h, c: (0, 1, 0, 0, h))
    qs = pl.BlockSpec((2, n, 1, pr, HEAD_DIM), lambda h, c: (0, 0, seq, 0, h))
    table = pl.BlockSpec((2, n, 1, pr, HEAD_DIM), lambda h, c: (0, 0, seq, 0, 0))
    kv_out = pl.BlockSpec((ctx_count, 2, 2, span, HEAD_DIM), lambda h, c: (0, 0, 0, 0, h))
    held = ([] if out is None else [out]) + list(deps)
    return pl.pallas_call(
        functools.partial(attend_back_kernel, ctx_count),
        grid_spec=pltpu.PrefetchScalarGridSpec(
            num_scalar_prefetch=1,
            grid=(heads,),
            in_specs=[
                qs,
                ks,
                vs,
                qs,
                qs,
                pl.BlockSpec((1, 2, 8, span), lambda h, c: (h, 0, 0, 0)),
                table,
                table,
                pl.BlockSpec((2, span, 1), lambda h, c: (0, 0, 0)),
                pl.BlockSpec((2, 1, span), lambda h, c: (0, 0, 0)),
            ]
            + [pl.BlockSpec(memory_space=pl.ANY)] * len(held),
            out_specs=[qs, kv_out],
            scratch_shapes=[
                pltpu.VMEM((ctx_count, 2, span, HEAD_DIM), F32),
                pltpu.VMEM((ctx_count, 2, span, HEAD_DIM), F32),
                pltpu.VMEM((span, HEAD_DIM), F32),
            ],
        ),
        out_shape=[jax.ShapeDtypeStruct(q.shape, BF), jax.ShapeDtypeStruct(kv.shape, BF)],
        input_output_aliases={} if out is None else {11: 0},
        compiler_params=pltpu.CompilerParams(vmem_limit_bytes=56 * MIB),
        cost_estimate=pl.CostEstimate(
            flops=heads * 9 * 20 * span * span * HEAD_DIM, bytes_accessed=12 * MIB, transcendentals=0
        ),
        name="attend_back",
    )(c, q, kv, kv, do, o, lse, cosine, sine, flag_col, flag_row, *held)


def merge_kernel(n, ctx_count, c_ref, shard_ref, *refs):
    a_refs, b_refs, refs = refs[:n], refs[n : 2 * n], refs[2 * n :]
    pieces, refs = refs[:ctx_count], refs[ctx_count:]
    h_ref, gain_ref, r_ref, n_ref, own_ref, logit_ref, w_ref, mixed_ref, wide = refs
    i = pl.program_id(0)
    c = c_ref[0]
    count, local = wide.shape[0], wide.shape[1] // n
    own, tile, share = count // n, h_ref.shape[0], local // ctx_count
    per_span = count // tile

    @pl.when(i == 0)
    def _():
        half = ctx_count // 2
        for j in range(ctx_count):
            other = lax.rem(c // 2 - j // 2 + half, half) * 2 + lax.rem(c + j, 2)
            at = pl.multiple_of(other * share, share)
            for k in range(n):
                w_ref[k, pl.ds(at, share), :] = pieces[j][shard_ref[k]]

    def turned(ref, k, by):
        cols = slice(k * local, (k + 1) * local)
        wide[by * own :, cols] = ref[: count - by * own]
        if by:
            wide[: by * own, cols] = ref[count - by * own : count]

    @pl.when(i == 0)
    def _():
        for k in range(n):
            turned(a_refs[k], k, k)

    @pl.when(i == per_span)
    def _():
        for k in range(n):
            turned(b_refs[-k % n], k, -k % n)

    part = lax.rem(i, per_span)
    rows = wide[pl.ds(pl.multiple_of(part * tile, tile), tile), :]
    weights = w_ref[...].reshape(n * local, w_ref.shape[2])
    resid = h_ref[...].astype(F32) + dot(rows, weights, 1, 0)
    inverse = lax.rsqrt(jnp.mean(resid * resid, axis=-1, keepdims=True) + EPSILON)
    normed = (resid * inverse * gain_ref[...]).astype(BF)
    n_ref[...] = normed
    logit_ref[...] = dot(r_ref[...], normed, 1, 1)

    @pl.when(part == 0)
    def _():
        own_ref[0] = resid[:own]
        mixed_ref[0] = rows[:own]


def merge(c, shards, got_a, got_b, pieces, rows, gain, router_t):
    count, width = rows.shape
    n, ctx_count = len(got_a), len(pieces)
    span, local = got_b[0].shape
    tile = 256
    per_span, own = span // tile, span // n
    once = pl.Buffered(1)
    row = pl.BlockSpec((tile, width), lambda i, c, f: (i, 0))
    own_rows = pl.BlockSpec((1, own, width), lambda i, c, f: (i // per_span, 0, 0))
    whole = lambda shape: pl.BlockSpec(
        shape, lambda i, c, f: (0,) * len(shape), pipeline_mode=once
    )
    return pl.pallas_call(
        functools.partial(merge_kernel, n, ctx_count),
        grid_spec=pltpu.PrefetchScalarGridSpec(
            num_scalar_prefetch=2,
            grid=(count // tile,),
            in_specs=[whole((span, local))] * (2 * n)
            + [whole(pieces[0].shape)] * ctx_count
            + [row, whole((1, width)), whole(router_t.shape)],
            out_specs=[
                row,
                own_rows,
                pl.BlockSpec((router_t.shape[0], tile), lambda i, c, f: (0, i)),
                whole((n, local, width)),
                own_rows,
            ],
            scratch_shapes=[pltpu.VMEM((span, width), BF)],
        ),
        out_shape=[
            jax.ShapeDtypeStruct((count, width), BF),
            jax.ShapeDtypeStruct((count // span, own, width), F32),
            jax.ShapeDtypeStruct((router_t.shape[0], count), F32),
            jax.ShapeDtypeStruct((n, local, width), BF),
            jax.ShapeDtypeStruct((count // span, own, width), BF),
        ],
        compiler_params=pltpu.CompilerParams(vmem_limit_bytes=60 * MIB),
        cost_estimate=pl.CostEstimate(
            flops=2 * count * width * width, bytes_accessed=8 * count * width, transcendentals=0
        ),
        name="merge",
    )(c, shards, *got_a, *got_b, *pieces, rows, gain, router_t)


def project_back_kernel(seqs, dq_ref, *refs):
    pairs, refs = refs[:seqs], refs[seqs:]
    cos_ref, sin_ref, w_ref, h_ref, raw_ref, gn_ref, gain_ref = refs
    x = h_ref[...].astype(F32)
    inverse = lax.rsqrt(jnp.mean(x * x, axis=-1, keepdims=True) + EPSILON)
    cosine, sine = cos_ref[...], sin_ref[...]
    _, _, blocks, pr, local = pairs[0].shape
    raw_ref[0] = dq_ref[...]
    for b in range(blocks):
        for s in range(seqs):
            at = slice((b * seqs + s) * pr, (b * seqs + s + 1) * pr)
            raw_ref[2, at] = pairs[s][1, 0, b].astype(BF)
            for lo in range(0, local, HEAD_DIM):
                cols = slice(lo, lo + HEAD_DIM)
                part = pairs[s][0, 0, b, :, cols].astype(F32)
                part = part * cosine[at] - pltpu.roll(part, HEAD_DIM // 2, 1) * sine[at]
                raw_ref[1, at, cols] = part.astype(BF)
    gn = dot(raw_ref[0], w_ref[0], 1, 1)
    gn += dot(raw_ref[1], w_ref[1], 1, 1)
    gn += dot(raw_ref[2], w_ref[2], 1, 1)
    gn_ref[...] = gn.astype(BF)
    part = jnp.sum((gn * x * inverse).reshape(-1, 8, x.shape[1]), axis=0)

    @pl.when(pl.program_id(0) == 0)
    def _():
        gain_ref[...] = part

    @pl.when(pl.program_id(0) != 0)
    def _():
        gain_ref[...] += part


def project_back(dq, pairs, cosine, sine, weights, rows):
    count, width = rows.shape
    local = weights.shape[2]
    seqs = len(pairs)
    _, _, n, pr, _ = pairs[0].shape
    tile = 256
    blocks = tile // (seqs * pr)
    per_span = n // blocks
    row = lambda w: pl.BlockSpec((tile, w), lambda i: (i, 0))
    pair = pl.BlockSpec(
        (2, 1, blocks, pr, local), lambda i: (0, i // per_span, lax.rem(i, per_span), 0, 0)
    )
    return pl.pallas_call(
        functools.partial(project_back_kernel, seqs),
        grid=(count // tile,),
        in_specs=[row(local)]
        + [pair] * seqs
        + [
            row(HEAD_DIM),
            row(HEAD_DIM),
            pl.BlockSpec((3, width, local), lambda i: (0, 0, 0)),
            row(width),
        ],
        out_specs=[
            pl.BlockSpec((3, tile, local), lambda i: (0, i, 0)),
            row(width),
            pl.BlockSpec((8, width), lambda i: (0, 0)),
        ],
        out_shape=[
            jax.ShapeDtypeStruct((3, count, local), BF),
            jax.ShapeDtypeStruct((count, width), BF),
            jax.ShapeDtypeStruct((8, width), F32),
        ],
        compiler_params=pltpu.CompilerParams(vmem_limit_bytes=48 * MIB),
        cost_estimate=pl.CostEstimate(
            flops=6 * count * width * local, bytes_accessed=6 * count * width, transcendentals=0
        ),
        name="project_back",
    )(dq, *pairs, cosine, sine, weights, rows)


def spread(ref, rows):
    lead = ref.shape[:-2]
    if ref.shape[-2] % 16 == 0 or not lead:
        return [ref[...].reshape(rows, ref.shape[-1])]
    return [ref[index] for index in np.ndindex(*lead)]


def inner_kernel(expert_tiles, blocks, shard_ref, x_ref, *refs):
    c_refs, refs = refs[:blocks], refs[blocks:]
    mix_ref, ei_ref, si_ref, eo_ref, so_ref, d_ref, act_ref, dot_ref, c_all = refs
    k = pl.program_id(0)
    x_rows, c_rows = x_ref.shape[0], 256
    cut = c_refs[0].shape[2]

    @pl.when(k == 0)
    def _():
        for m in range(blocks):
            c_all[m * cut : (m + 1) * cut] = c_refs[m][0, 0]

    rows_in, rows_out = d_ref.shape[1], act_ref.shape[1]

    def finish(h_gate, h_up, u, scale):
        sig = 1.0 / (1.0 + jnp.exp(-h_gate))
        silu = h_gate * sig
        act = silu * h_up
        gu = u * scale
        d_gate = gu * h_up * sig * (1.0 + h_gate * (1.0 - sig))
        dots = jnp.sum(act * u, axis=0, keepdims=True)
        return (act * scale).astype(BF), d_gate.astype(BF), (gu * silu).astype(BF), dots

    def run(w_in, w_out, groups):
        size = rows_out // groups
        for lo in range(0, x_rows, c_rows):
            cols = slice(lo, lo + c_rows)
            xt, ct = x_ref[cols], c_all[cols]
            h = jnp.concatenate([dot(w, xt, 1, 1) for w in spread(w_in, rows_in)])
            u = jnp.concatenate([dot(w, ct, 1, 1) for w in spread(w_out, rows_out)])
            for g in range(groups):
                at = g * 2 * size
                act, dg, du, dots = finish(
                    h[at : at + size],
                    h[at + size : at + 2 * size],
                    u[g * size : (g + 1) * size],
                    mix_ref[0, g : g + 1, cols],
                )
                act_ref[0, g * size : (g + 1) * size, cols] = act
                d_ref[0, at : at + size, cols] = dg
                d_ref[0, at + size : at + 2 * size, cols] = du
                dot_ref[0, g : g + 1, cols] = dots

    @pl.when(k < expert_tiles)
    def _():
        run(ei_ref, eo_ref, 2)

    @pl.when(k >= expert_tiles)
    def _():
        run(si_ref, so_ref, 1)


def tile_specs(expert_in, shared_in, expert_out, shared_out, index, width):
    experts, _, f, _ = expert_in.shape
    last, share = experts // 2 - 1, 2 * f
    lo = lambda *i: jnp.minimum(index(*i), last)
    hi = lambda *i: jnp.maximum(index(*i) - last - 1, 0)
    return (
        pl.BlockSpec((2, 2, f, width), lambda *i: (lo(*i), 0, 0, 0)),
        pl.BlockSpec((2, share, width), lambda *i: (0, hi(*i), 0)),
        pl.BlockSpec((2, f, width), lambda *i: (lo(*i), 0, 0)),
        pl.BlockSpec((share, width), lambda *i: (hi(*i), 0)),
    )


def block_specs(n, cut, width):
    return [
        pl.BlockSpec(
            (1, 1, cut, width),
            lambda i, *p, t=t, k=k: (p[-1][t * n + k], t, 0, 0),
            pipeline_mode=pl.Buffered(1),
        )
        for t in range(2)
        for k in range(n)
    ]


def inner(shards, x, cot, mix, weights):
    rows, width = x.shape
    n, _, cut, _ = cot.shape
    expert_in, shared_in, expert_out, shared_out = weights
    f = expert_in.shape[2]
    tiles = expert_in.shape[0] // 2 + shared_out.shape[0] // (2 * f)
    whole = pl.BlockSpec((rows, width), lambda i, p: (0, 0), pipeline_mode=pl.Buffered(1))
    out = lambda r: pl.BlockSpec((1, r, rows), lambda i, p: (i, 0, 0))
    return pl.pallas_call(
        functools.partial(inner_kernel, expert_in.shape[0] // 2, 2 * n),
        grid_spec=pltpu.PrefetchScalarGridSpec(
            num_scalar_prefetch=1,
            grid=(tiles,),
            in_specs=[whole]
            + block_specs(n, cut, width)
            + [out(8), *tile_specs(*weights, lambda i, p: i, width)],
            out_specs=[out(4 * f), out(2 * f), out(8)],
            scratch_shapes=[pltpu.VMEM((rows, width), BF)],
        ),
        out_shape=[
            jax.ShapeDtypeStruct((tiles, 4 * f, rows), BF),
            jax.ShapeDtypeStruct((tiles, 2 * f, rows), BF),
            jax.ShapeDtypeStruct((tiles, 8, rows), F32),
        ],
        compiler_params=pltpu.CompilerParams(vmem_limit_bytes=62 * MIB),
        cost_estimate=pl.CostEstimate(
            flops=12 * f * rows * width * tiles,
            bytes_accessed=12 * f * width * tiles + 4 * rows * width,
            transcendentals=0,
        ),
        name="inner",
    )(shards, x, *[cot] * (2 * n), mix, *weights)


def outer_kernel(expert_tiles, shard_ref, d_ref, e_ref, s_ref, *refs):
    o_ref, acc = refs[-2:]
    k = pl.program_id(1)
    n, _, cut, _ = o_ref.shape

    @pl.when(k == 0)
    def _():
        acc[...] = jnp.zeros_like(acc)

    def run(w_ref):
        units = d_ref.shape[0] * d_ref.shape[1]
        hid = d_ref[...].reshape(units, d_ref.shape[2])
        at = 0
        for w in spread(w_ref, units):
            for lo in range(0, acc.shape[1], 512):
                acc[:, lo : lo + 512] += dot(
                    hid[at : at + w.shape[0]], w[:, lo : lo + 512], 0, 0
                )
            at += w.shape[0]

    @pl.when(k < expert_tiles)
    def _():
        run(e_ref)

    @pl.when(k >= expert_tiles)
    def _():
        run(s_ref)

    @pl.when(k == pl.num_programs(1) - 1)
    def _():
        first = pl.program_id(0) * n
        for m in range(n):
            to = m if shard_ref is None else shard_ref[first + m]
            o_ref[to, 0] = acc[m * cut : (m + 1) * cut].astype(BF)


def outer(shards, n, hid, expert, shared, *deps):
    tiles, units, tokens = hid.shape
    width, f = expert.shape[-1], expert.shape[-2]
    rows = tokens // 2
    if expert.ndim == 4:
        group, step = 1, 2
        e_shape, s_shape = (2, 2, f, width), (2, 2 * f, width)
    else:
        group, step = 2, 4
        e_shape, s_shape = (4, f, width), (4 * f, width)
    last = expert.shape[0] // step - 1
    lo = lambda k: jnp.minimum(k, last)
    hi = lambda k: jnp.maximum(k - last - 1, 0)
    if expert.ndim == 4:
        e_spec = pl.BlockSpec(e_shape, lambda t, k, *p: (lo(k), 0, 0, 0))
        s_spec = pl.BlockSpec(s_shape, lambda t, k, *p: (0, hi(k), 0))
    else:
        e_spec = pl.BlockSpec(e_shape, lambda t, k, *p: (lo(k), 0, 0))
        s_spec = pl.BlockSpec(s_shape, lambda t, k, *p: (hi(k), 0))
    return pl.pallas_call(
        functools.partial(outer_kernel, last + 1)
        if shards is not None
        else functools.partial(outer_kernel, last + 1, None),
        grid_spec=pltpu.PrefetchScalarGridSpec(
            num_scalar_prefetch=0 if shards is None else 1,
            grid=(2, tiles // group),
            in_specs=[pl.BlockSpec((group, units, rows), lambda t, k, *p: (k, 0, t)), e_spec, s_spec]
        + [pl.BlockSpec(memory_space=pl.ANY)] * len(deps),
            out_specs=pl.BlockSpec((n, 1, rows // n, width), lambda t, k, *p: (0, t, 0, 0)),
            scratch_shapes=[pltpu.VMEM((rows, width), F32)],
        ),
        out_shape=jax.ShapeDtypeStruct((n, 2, rows // n, width), BF),
        compiler_params=pltpu.CompilerParams(vmem_limit_bytes=58 * MIB),
        cost_estimate=pl.CostEstimate(
            flops=2 * tiles * units * tokens * width,
            bytes_accessed=2 * tiles * units * (tokens + 2 * width) + 2 * tokens * width,
            transcendentals=0,
        ),
        name="outer",
    )(*([] if shards is None else [shards]), hid, expert, shared, *deps)


def weight_kernel(blocks, core_ref, shard_ref, h_ref, *refs):
    def run(o_ref):
        for lo in range(0, o_ref.shape[1], 512):
            cols = slice(lo, lo + 512)
            if blocks:
                other = jnp.concatenate([ref[0, 0, :, cols] for ref in refs[:blocks]])
            else:
                other = refs[0][:, cols]
            o_ref[:, cols] = dot(h_ref[0], other, 1, 0).astype(BF)

    @pl.when(pl.program_id(0) == core_ref[0])
    def _():
        run(refs[-2])

    @pl.when(pl.program_id(0) != core_ref[0])
    def _():
        run(refs[-1])


def weight_grad(core, shards, hid, other, base, stride, piece, pieces, *deps):
    _, units, tokens = hid.shape
    units = units // pieces
    width = other.shape[-1]
    if other.ndim == 4:
        specs = block_specs(other.shape[0], other.shape[2], width)
    else:
        specs = [
            pl.BlockSpec((tokens, width), lambda i, c, p: (0, 0), pipeline_mode=pl.Buffered(1))
        ]
    return pl.pallas_call(
        functools.partial(weight_kernel, len(specs) if other.ndim == 4 else 0),
        grid_spec=pltpu.PrefetchScalarGridSpec(
            num_scalar_prefetch=2,
            grid=(2,),
            in_specs=[
                pl.BlockSpec((1, units, tokens), lambda i, c, p: (base + stride * i, piece, 0)),
            ]
            + specs
            + [pl.BlockSpec(memory_space=pl.ANY)] * len(deps),
            out_specs=[pl.BlockSpec((units, width), lambda i, c, p: (0, 0))] * 2,
        ),
        out_shape=[jax.ShapeDtypeStruct((units, width), BF)] * 2,
        compiler_params=pltpu.CompilerParams(vmem_limit_bytes=40 * MIB),
        cost_estimate=pl.CostEstimate(
            flops=4 * units * tokens * width,
            bytes_accessed=4 * units * (tokens + width) + 2 * tokens * width,
            transcendentals=0,
        ),
        name="weight_grad",
    )(core, shards, hid, *[other] * len(specs), *deps)


def finish_kernel(core_ref, *refs):
    o_ref = refs[-1]
    which = pl.program_id(0) * pl.num_programs(1) + pl.program_id(1)
    for m, ref in enumerate(refs[:-1]):

        @pl.when(which == m)
        def _(ref=ref):
            o_ref[...] = ref[...].astype(F32).reshape(o_ref.shape)


def finish(core, kept, got, gated):
    count = len(kept)
    rows, width = kept[0].shape
    tile = rows // 2 if rows % 32 == 0 else rows
    steps = rows // tile
    at = lambda m: lambda h, j, r, c: (
        jnp.where(h * count + j == m, r, jnp.where(h * count + j < m, 0, steps - 1)),
        0,
    )
    if gated:
        shape = (count, 2, rows, width)
        place = lambda h, j, r, c: (j, lax.rem(h + c[0], 2), r, 0)
    else:
        shape = (2, count, rows, width)
        place = lambda h, j, r, c: (lax.rem(h + c[0], 2), j, r, 0)
    return pl.pallas_call(
        finish_kernel,
        grid_spec=pltpu.PrefetchScalarGridSpec(
            num_scalar_prefetch=1,
            grid=(2, count, steps),
            in_specs=[pl.BlockSpec((tile, width), at(m)) for m in range(2 * count)],
            out_specs=pl.BlockSpec((1, 1, tile, width), place),
        ),
        out_shape=jax.ShapeDtypeStruct(shape, F32),
        compiler_params=pltpu.CompilerParams(vmem_limit_bytes=40 * MIB),
        cost_estimate=pl.CostEstimate(
            flops=0, bytes_accessed=12 * count * rows * width, transcendentals=0
        ),
        name="finish",
    )(core, *kept, *got)


class Ring:
    def __init__(self, count):
        self.count = count
        self.order = ring_order(count)
        self.place = np.argsort(np.array(self.order))

    def shift(self, value, by):
        n = self.count
        pairs = [(self.order[i], self.order[(i + by) % n]) for i in range(n)]
        return lax.ppermute(value, "fsdp", pairs)

    def gather(self, ahead, behind, first=()):
        a, b = [ahead], [behind]
        for k in range(self.count - 1):
            to_a, to_b = a[-1], b[-1]
            if k == 1 and first:
                to_a, to_b = after(to_a, *first), after(to_b, *first)
            a.append(self.shift(to_a, 1))
            b.append(self.shift(to_b, -1))
        return a, b

    def scatter(self, ahead, behind, work=(), first=()):
        n = self.count
        a, b = ahead(1), behind(1)
        if first:
            a, b = after(a, *first), after(b, *first)
        held = []
        for k in range(2, n + 1):
            kind = BF if k < n else F32
            a = (self.shift(a, 1).astype(F32) + ahead(k % n).astype(F32)).astype(kind)
            b = (self.shift(b, -1).astype(F32) + behind(k % n).astype(F32)).astype(kind)
            if held:
                a, b = after(a, *held), after(b, *held)
            held = work(k, a, b) if work else []
        return a, b, held


def ctx_pairs(ctx_count, lanes, core):
    half = ctx_count // 2
    return [(x * 2 + k, ((x + lanes) % half) * 2 + (k ^ core)) for x in range(half) for k in range(2)]


def ctx_gather(value, ctx_count, *ties):
    got = []
    for lanes in range(ctx_count // 2):
        mine = value
        if lanes:
            sent = after(value, *ties) if ties else value
            mine = lax.ppermute(sent, "ctx", ctx_pairs(ctx_count, lanes, 0))
        got.append(mine)
        got.append(lax.ppermute(mine, "ctx", ctx_pairs(ctx_count, 0, 1)))
    return got


def ctx_scatter(parts, ctx_count):
    half = ctx_count // 2
    total = None
    for lanes in reversed(range(half)):
        other = lax.ppermute(parts[2 * lanes + 1], "ctx", ctx_pairs(ctx_count, 0, 1))
        s = parts[2 * lanes].astype(F32) + other.astype(F32)
        if lanes:
            s = lax.ppermute(s.astype(BF), "ctx", ctx_pairs(ctx_count, -lanes % half, 0)).astype(F32)
        total = s if total is None else total + s
    return total


class Sum:
    def __init__(self, value):
        self.value = value

    def reduce(self):
        flip = ctx_pairs(4, 0, 1)
        keep, send = self.value[0], self.value[1]
        self.part = (keep.astype(F32) + lax.ppermute(send, "ctx", flip).astype(F32)).astype(BF)
        return self.part

    def cross(self, *ties):
        part = after(self.part, *ties) if ties else self.part
        self.got = lax.ppermute(part, "ctx", ctx_pairs(4, 1, 0))
        return self.got

    def finish(self, *ties):
        got = after(self.got, *ties) if ties else self.got
        t = (self.part.astype(F32) + got.astype(F32)).astype(BF)
        return t, lax.ppermute(t, "ctx", ctx_pairs(4, 0, 1))


def kept_table(route_rows, keys, experts, capacity):
    index = jnp.arange(keys.shape[0], dtype=jnp.int32)
    before = (keys[None, :] < keys[:, None]) | (
        (keys[None, :] == keys[:, None]) & (index[None, :] < index[:, None])
    )
    named = jnp.any(
        route_rows[None, :, :] == jnp.arange(experts, dtype=jnp.int32)[:, None, None], axis=2
    )
    ahead = dot(named.astype(BF), before.astype(BF), 1, 1)
    return (named & (ahead < capacity)).astype(BF)


def per_device(
    hidden_in,
    cotangent,
    routes,
    priority,
    gain_attn,
    attention_input_weights,
    attention_output_weights,
    gain_ffn,
    router,
    shared_gate,
    shared_in,
    shared_out,
    expert_in,
    expert_out,
):
    n = lax.axis_size("fsdp")
    ctx_count = lax.axis_size("ctx")
    c = lax.axis_index("ctx")
    core = lax.rem(c, 2)
    ring = Ring(n)
    place = jnp.asarray(ring.place, jnp.int32)[lax.axis_index("fsdp")]
    seqs, _, _, pr, width = hidden_in.shape
    span = pr * n
    local = attention_input_weights.shape[2]
    experts = expert_in.shape[0]
    top = routes.shape[-1]
    own_rows = seqs * 2 * pr
    tokens = own_rows * n
    capacity = 5 * own_rows * top // (4 * experts)
    slices = width // n

    cut = seqs * pr
    hidden = jnp.transpose(hidden_in[:, :, 0], (1, 0, 2, 3)).reshape(2, cut, width)

    def as_rows(value):
        value = value.reshape(-1)
        return jnp.pad(value, (0, 8 * width - value.size)).reshape(8, width)

    small = jnp.concatenate([gain_attn[None], gain_ffn[None], shared_gate[None], router.T])
    small_count = small.shape[0]
    got_a, got_b = ring.gather(jnp.concatenate([hidden[0], as_rows(small)]), hidden[1])
    last = got_a[-1], got_b[-1]
    places = jnp.asarray(ring.place, jnp.int32)
    order = jnp.asarray(ring.order, jnp.int32)
    steps = jnp.arange(n, dtype=jnp.int32)
    place = after(place, got_a[2])
    by_shard = (place - places) % n
    shards = jnp.stack([order[(place - steps) % n], order[(place + steps) % n]])
    offset = shards[:, :, None] * pr + jnp.arange(pr, dtype=jnp.int32)
    c_later = after(c, got_a[3])
    start = jnp.stack([c_later, 2 * ctx_count - 1 - c_later]) * span
    positions = start[:, None, None] + offset
    flags = (offset // BLOCK).astype(F32).reshape(2, span)
    flag_col, flag_row = flags[:, :, None], flags[:, None, :]
    halves = jnp.arange(HEAD_DIM, dtype=jnp.int32) % (HEAD_DIM // 2)
    frequency = ROPE_BASE ** (-2.0 * halves.astype(F32) / HEAD_DIM)
    angles = positions.astype(F32)[..., None] * frequency
    sign = jnp.where(jnp.arange(HEAD_DIM) < HEAD_DIM // 2, -1.0, 1.0)
    by_seq = (2, n, seqs, pr, HEAD_DIM)
    cosine = jnp.broadcast_to(jnp.cos(angles)[:, :, None], by_seq)
    sine = jnp.broadcast_to((jnp.sin(angles) * sign)[:, :, None], by_seq)
    flat_cos, flat_sin = cosine.reshape(tokens, HEAD_DIM), sine.reshape(tokens, HEAD_DIM)

    shard_list = shards.reshape(-1)
    c_arr = c.reshape(1).astype(jnp.int32)
    core_arr = core.reshape(1).astype(jnp.int32)
    smalls = jnp.stack([g[cut:].reshape(-1)[: small.size] for g in got_a])
    smalls = smalls.reshape(n, small_count, slices)
    smalls = jnp.take(smalls, by_shard, axis=0)
    smalls = jnp.transpose(smalls, (1, 0, 2)).reshape(small_count, width)
    all_rows = jnp.concatenate([g[:cut] for g in got_a] + got_b)
    gain_one, gain_two = smalls[0:1].astype(F32), smalls[1:2].astype(F32)
    logit_rows = jnp.concatenate(
        [smalls[3:], smalls[2:3], jnp.zeros((16 - experts - 1, width), BF)]
    )

    share = local // ctx_count
    mine = lax.dynamic_slice_in_dim(attention_output_weights, c * share, share, 0)
    out_piece = lax.all_gather(after(mine, got_a[n - 2], got_b[n - 2]), "fsdp", axis=0)
    cot = jnp.transpose(cotangent[:, :, 0], (1, 0, 2, 3)).reshape(2, cut, width)
    cot_all = lax.all_gather(after(cot, *last), "fsdp", axis=0)
    routes_in, priority_in = after(routes, got_a[5]), after(priority, got_a[5])
    kept_own = kept_table(
        routes_in.reshape(own_rows, top), priority_in.reshape(own_rows), experts, capacity
    )
    kept_fill = -(-kept_own.size // local) % 8
    kept_rows = jnp.pad(kept_own.reshape(-1, local), ((0, kept_fill and 8 - kept_fill), (0, 0)))

    normed_one, query, kv_own = project(
        all_rows, gain_one, attention_input_weights, flat_cos, flat_sin, seqs, n
    )
    query = query.reshape(2, n, seqs, pr, local)
    pieces = [ctx_gather(kv_own[0], ctx_count)]
    for s in range(1, seqs):
        pieces.append(ctx_gather(kv_own[s], ctx_count, pieces[-1][2]))
    kvs = []
    mixed, log_sums = None, []
    for s in range(seqs):
        if s:
            pieces[s] = [after(piece, mixed) for piece in pieces[s]]
        kvs.append(jnp.stack(pieces[s]).reshape(ctx_count, 2, 2, span, local))
        mixed, lse = attend(c_arr, query, kvs[s], s, flag_col, flag_row, mixed)
        log_sums.append(lse)
    sent = mixed.reshape(2, tokens // 2, local)
    sent_after = mixed
    got_a, got_b = ring.gather(
        jnp.concatenate([sent[0], kept_rows]), sent[1], [cot_all]
    )
    out_pieces = ctx_gather(after(out_piece, sent_after), ctx_count)
    kept = [
        g[tokens // 2 :].reshape(-1)[: kept_own.size].reshape(experts, seqs, 2, pr) for g in got_a
    ]
    kept = jnp.stack(
        [
            jnp.stack([g[:, :, 0] for g in kept], axis=1),
            jnp.stack([kept[(n - k) % n][:, :, 1] for k in range(n)], axis=1),
        ],
        axis=1,
    )
    kept = kept.reshape(experts, tokens).astype(F32)
    x, resid, logit, out_full, mixed_own = merge(
        c_arr, shard_list, got_a, got_b, out_pieces, all_rows, gain_two, logit_rows
    )
    out_full = out_full.reshape(width, width)
    resid = resid.reshape(own_rows, width)

    top_logit = jnp.max(logit[:experts], axis=0, keepdims=True)
    raised = jnp.exp(logit[:experts] - top_logit)
    gates = raised / jnp.sum(raised, axis=0, keepdims=True)
    weight_s = jax.nn.sigmoid(logit[experts : experts + 1])
    small_tiles = shared_out.shape[0] // (2 * expert_in.shape[2])
    mix = jnp.concatenate(
        [
            jnp.pad((gates * kept).reshape(experts // 2, 2, tokens), ((0, 0), (0, 6), (0, 0))),
            jnp.broadcast_to(jnp.pad(weight_s, ((0, 7), (0, 0)))[None], (small_tiles, 8, tokens)),
        ]
    )
    d_buf, act_buf, dots = inner(
        shard_list, x, cot_all, mix, (expert_in, shared_in, expert_out, shared_out)
    )
    split = lambda value: value.reshape(2, n, cut, width)
    dots_e = dots[: experts // 2, :2].reshape(experts, tokens) * kept
    dots_s = jnp.sum(dots[experts // 2 :, 0], axis=0, keepdims=True)
    dots = jnp.concatenate([dots_e, dots_s, jnp.zeros((7, tokens), F32)])
    dots = dots.reshape(16, 2, n, cut)
    dots = jnp.stack(
        [jnp.take(dots[:, 0], by_shard, axis=1), jnp.take(dots[:, 1], -by_shard % n, axis=1)],
        axis=2,
    )
    dots = jnp.transpose(dots, (1, 0, 2, 3)).reshape(n, 16, own_rows)
    dot_own = lax.psum_scatter(dots, "fsdp", scatter_dimension=0, tiled=True)[0]

    f = expert_in.shape[2]
    quarter = experts // 4
    halves = small_tiles // 2
    four = ctx_count == 4
    spots = [(j, quarter) for j in range(quarter)] + [
        (experts // 2 + j, halves) for j in range(halves)
    ]
    sums = {}

    def weight_piece(key, *ties):
        name, base, piece = key
        buf, other = (d_buf, x) if name == "in" else (act_buf, cot_all)
        sums[key] = Sum(
            weight_grad(
                core_arr,
                shard_list,
                buf,
                other,
                base,
                dict(spots)[base],
                piece,
                2 if name == "in" else 1,
                *ties,
            )
        )
        return sums[key].value[0]

    late = [("out", base, 0) for base, _ in spots]
    queue = [("in", base, piece) for base, _ in spots for piece in (0, 1)]
    beside_in, after_in = queue[:-1], queue[-1:]
    flown = []

    def fly(key):
        if four:
            sums[key].reduce()
            flown.append(sums[key].cross(*flown[-2:-1]))
            return [flown[-1]]
        return []

    early = []
    for key in late[:2]:
        early.append(weight_piece(key))
    early_got = [fly(key) for key in late[:2]]
    if four:
        early = [sums[key].part for key in late[:2]]
    grad_in = outer(None, n, d_buf, expert_in, shared_in, *early)

    def beside(k, a, b):
        held = []
        if k - 2 < len(beside_in):
            held.append(weight_piece(beside_in[k - 2], a, b))
        if four and 0 <= k - 3 < len(beside_in):
            held.append(sums[beside_in[k - 3]].reduce())
            flown.append(sums[beside_in[k - 3]].cross(*flown[-2:-1]))
        if k == 3:
            held += early_got[1]
        if k == n - 1 and four:
            held.append(sums[beside_in[0]].got)
        return held

    gi_a, gi_b, _ = ring.scatter(
        lambda k: grad_in[k, 0], lambda k: grad_in[k, 1], beside, early_got[0]
    )
    for key in beside_in[n - 1 :]:
        weight_piece(key, gi_a, gi_b)
    if four:
        for key in beside_in[n - 2 :]:
            sums[key].reduce()
            flown.append(sums[key].cross(*flown[-2:-1]))
    got_in = [sums[key].got for key in beside_in] if four else []

    def norm_back(grad, value, gain):
        inverse = lax.rsqrt(jnp.mean(value * value, axis=-1, keepdims=True) + EPSILON)
        scaled = grad * gain
        return inverse * (
            scaled - value * inverse * inverse * jnp.mean(scaled * value, axis=-1, keepdims=True)
        ), inverse

    own_of = lambda value: value.reshape(-1, 2, n, cut)[:, :, 0].reshape(-1, own_rows)
    gates_own, weight_own = own_of(gates), own_of(weight_s)
    x_own = split(x)[:, 0].reshape(own_rows, width)
    d_gates = dot_own[:experts]
    d_logit = (
        gates_own * (d_gates - jnp.sum(gates_own * d_gates, axis=0, keepdims=True))
    ).astype(BF)
    d_gate_s = dot_own[experts : experts + 1] * weight_own * (1.0 - weight_own)
    d_rows = jnp.concatenate([d_gate_s, d_logit.astype(F32)])
    grad_n2 = jnp.concatenate([gi_a, gi_b])
    grad_n2 = grad_n2 + jnp.einsum("er,ed->rd", d_rows, smalls[2:].astype(F32), precision=EXACT)
    grad_small = jnp.einsum("er,rd->ed", d_rows, x_own.astype(F32), precision=EXACT)
    back, inverse_two = norm_back(grad_n2, resid, gain_two)
    grad_gain_two = jnp.sum(grad_n2 * resid * inverse_two, axis=0, keepdims=True)
    grad_mid = cot.reshape(own_rows, width).astype(F32) + back
    branch = grad_mid.astype(BF)

    grad_mixed = dot(branch, out_full, 1, 1).astype(BF)
    grad_mixed = jnp.take(grad_mixed.reshape(own_rows, n, local), by_shard, axis=1)
    grad_mixed = jnp.transpose(grad_mixed, (1, 0, 2))
    out_part = outer(shard_list, n, act_buf, expert_out, shared_out, grad_mixed, *got_in[1:2])
    moved = lax.all_to_all(
        grad_mixed, "fsdp", split_axis=0, concat_axis=0, tiled=True
    ).reshape(n, 2, cut, local)
    d_o = jnp.concatenate(
        [jnp.take(moved[:, 0], shards[0], axis=0), jnp.take(moved[:, 1], shards[1], axis=0)]
    ).reshape(2, n, seqs, pr, local)
    d_o = after(d_o, out_part)

    in_place = lambda value: jnp.transpose(
        value.reshape(2, seqs, pr, width), (1, 0, 2, 3)
    ).reshape(hidden_in.shape)
    out_own = lax.psum_scatter(out_part, "fsdp", scatter_dimension=0, tiled=True)

    lo = range(quarter)
    hi = range(experts // 2, experts // 2 + halves)
    done = {}

    def finished(keys, gated, *ties):
        for key in keys:
            if key not in done:
                done[key] = sums[key].finish(*ties)
        kept_halves, got_halves = zip(*[done[key] for key in keys])
        return finish(core_arr, kept_halves, got_halves, gated)

    d_q, pairs = None, []
    if four:
        for key in beside_in[:2]:
            done[key] = sums[key].finish(out_part)
    for s in range(seqs):
        d_q, pair = attend_back(
            c_arr,
            query,
            kvs[s],
            d_o,
            mixed,
            log_sums[s],
            s,
            cosine,
            sine,
            flag_col,
            flag_row,
            d_q,
            *got_in[1 + s : 2 + s],
        )
        if s and four:
            pair = after(pair, *got_in[3:])
        pair = ctx_scatter([pair[j] for j in range(ctx_count)], ctx_count)
        pairs.append(pair.astype(BF).reshape(2, 2, n, pr, local))
    grad_out_own = dot(mixed_own.reshape(own_rows, width), branch, 0, 0).astype(BF)
    if four:
        flip, cross = ctx_pairs(4, 0, 1), ctx_pairs(4, 1, 0)
        lane = c // 2
        pick = lambda value, i, axis: lax.dynamic_index_in_dim(value, i, axis, keepdims=False)
        by_core = grad_out_own.reshape(n, 2, 2, share, width)
        part = pick(by_core, core, 2).astype(F32)
        part = part + lax.ppermute(pick(by_core, 1 - core, 2), "ctx", flip).astype(F32)
        part = part.astype(BF)
        quart_got = lax.ppermute(after(pick(part, 1 - lane, 1), *pairs), "ctx", cross)
    else:
        quart_got = lax.psum(grad_out_own, "ctx").reshape(n, local, width)
    for key in after_in + late[2:]:
        weight_piece(key, d_q)
        if four:
            sums[key].reduce()
            sums[key].cross(*pairs)
    if four:
        total_expert_in = finished([("in", j, p) for j in lo for p in (0, 1)], False, d_q)
        d_q = after(d_q, total_expert_in)

    raw, grad_n1, gain_part = project_back(
        d_q.reshape(tokens, local), pairs, flat_cos, flat_sin, attention_input_weights, all_rows
    )
    grad_n1 = split(grad_n1)
    grad_gain_one = jnp.sum(gain_part, axis=0, keepdims=True)
    smalls_back = jnp.concatenate(
        [grad_gain_one, grad_gain_two, grad_small, jnp.zeros((16 - small_count, width), F32)]
    )
    smalls_back = jnp.transpose(smalls_back.reshape(16, n, slices), (1, 0, 2))
    smalls_back = smalls_back.reshape(n, -1, width).astype(BF)
    small_rows = smalls_back.shape[1]
    smalls_back = jnp.pad(smalls_back, ((0, 0), (0, 8 - small_rows), (0, 0)))

    ended = {}

    def beside_last(k, a, b):
        held = []
        if k == 3:
            held.append(out_own)
        if k == 3:
            quart = after(quart_got, a)
            if four:
                quart = (pick(part, lane, 1).astype(F32) + quart.astype(F32)).astype(BF)
            quart = jnp.take(quart, by_shard, axis=0)
            quart = jnp.concatenate([quart, smalls_back], axis=1)
            ended["out"] = lax.psum_scatter(quart, "fsdp", scatter_dimension=0, tiled=True)[0]
        if k == n - 1 and four:
            held += [sums[key].got for key in after_in]
        return held

    gn_a, gn_b, _ = ring.scatter(lambda k: grad_n1[0, k], lambda k: grad_n1[1, k], beside_last)
    back_one, _ = norm_back(
        jnp.concatenate([gn_a, gn_b]), hidden.reshape(own_rows, width).astype(F32), gain_one
    )
    grad_hidden = in_place((grad_mid + back_one).astype(BF))
    out_own = after(out_own, gn_a, gn_b).reshape(own_rows, width).astype(F32)
    layer_out = in_place((resid + out_own).astype(BF))
    own_quart = after(ended["out"], gn_a, gn_b)
    small_own = own_quart[-8 : small_rows - 8].astype(F32).reshape(16, slices)
    own_quart = own_quart[:-8]
    if ctx_count == 4:
        small_own = small_own + lax.ppermute(small_own, "ctx", ctx_pairs(4, 0, 1))
        small_own = small_own + lax.ppermute(small_own, "ctx", ctx_pairs(4, 1, 0))
    else:
        small_own = lax.psum(small_own, "ctx")

    grad_attn_in = jnp.einsum("nd,jne->dje", normed_one, raw, preferred_element_type=F32)

    if ctx_count == 4:
        t = own_quart
        o = lax.ppermute(t, "ctx", cross)
        t = jnp.stack([jnp.where(lane == 0, t, o), jnp.where(lane == 0, o, t)])
        o = lax.ppermute(t, "ctx", flip)
        total_attn_out = jnp.stack(
            [jnp.where(core == 0, t, o), jnp.where(core == 0, o, t)], axis=1
        ).astype(F32)
    else:
        total_attn_out = own_quart.astype(F32)

    if four:

        def halved(value):
            keep = lax.dynamic_index_in_dim(value, core, 0, keepdims=False)
            send = lax.dynamic_index_in_dim(value, 1 - core, 0, keepdims=False)
            one = Sum((keep.astype(BF), send.astype(BF)))
            one.reduce()
            one.cross(*([sums[key].got for key in late[2:]]))
            t, o = one.finish(gn_a, gn_b)
            return jnp.stack([jnp.where(core == 0, t, o), jnp.where(core == 0, o, t)]).astype(F32)

        total_expert_out = finished([("out", j, 0) for j in lo], False, gn_a)
        total_shared_in = finished([("in", j, p) for j in hi for p in (0, 1)], True, gn_a)
        total_shared_out = finished([("out", j, 0) for j in hi], False, gn_a)
        total_attn_in = halved(grad_attn_in.reshape(2, width // 2, 3, local))
    else:
        first = core == 0

        def summed(keys, axis):
            values = [
                jnp.where(
                    first, jnp.stack(sums[key].value), jnp.stack(sums[key].value[::-1])
                )
                for key in keys
            ]
            return lax.psum(jnp.stack(values, axis=axis), "ctx").astype(F32)

        total_expert_in = summed([("in", j, p) for j in lo for p in (0, 1)], 1)
        total_expert_out = summed([("out", j, 0) for j in lo], 1)
        total_shared_in = summed([("in", j, p) for j in hi for p in (0, 1)], 0)
        total_shared_out = summed([("out", j, 0) for j in hi], 1)
        total_attn_in = lax.psum(grad_attn_in.astype(BF), "ctx").astype(F32)

    return (
        layer_out,
        grad_hidden,
        small_own[0],
        jnp.transpose(total_attn_in.reshape(width, 3, local), (1, 0, 2)),
        total_attn_out.reshape(local, width),
        small_own[1],
        small_own[3:small_count].T,
        small_own[2],
        total_shared_in.reshape(shared_in.shape),
        total_shared_out.reshape(shared_out.shape),
        total_expert_in.reshape(expert_in.shape),
        total_expert_out.reshape(expert_out.shape),
    )


def solution(mesh):
    rows = P(None, None, "ctx", "fsdp", None)
    return jax.shard_map(
        per_device,
        mesh=mesh,
        in_specs=(
            rows,
            rows,
            rows,
            P(None, None, "ctx", "fsdp"),
            P("fsdp"),
            P(None, None, "fsdp"),
            P("fsdp", None),
            P("fsdp"),
            P("fsdp", None),
            P("fsdp"),
            P(None, "fsdp", None),
            P("fsdp", None),
            P(None, None, "fsdp", None),
            P(None, "fsdp", None),
        ),
        out_specs=(
            rows,
            rows,
            P("fsdp"),
            P(None, None, "fsdp"),
            P("fsdp", None),
            P("fsdp"),
            P("fsdp", None),
            P("fsdp"),
            P(None, "fsdp", None),
            P("fsdp", None),
            P(None, None, "fsdp", None),
            P(None, "fsdp", None),
        ),
        check_vma=False,
    )
```
